256 devices in a mesh: section: 32 (over y, x, z_lo), tensor: 8 (over z_hi, core).
Axes of the slice: x: 4, y: 4, z: 8 (z_hi: 4, z_lo: 2; z = z_hi * 2 + z_lo), core: 2. Of those that a mesh axis runs over, the one named last changes fastest.
Arguments:
- layer_input: bfloat16 [32, 2, 256, 3072], P('section', None, None, 'tensor'), may hold values from -6 to 6
- upstream: bfloat16 [32, 2, 256, 3072], P('section', None, None, 'tensor'), may hold values from -6 to 6
- scores: bfloat16 [32, 2, 16, 256, 256], P('section', None, 'tensor'), may hold values from -12 to 260, as said below
- value_weight: bfloat16 [32, 3072, 2048], P('section', None, 'tensor'), may hold values from -0.109375 to 0.109375
- out_weight: bfloat16 [32, 2048, 3072], P('section', 'tensor'), may hold values from -0.125 to 0.125
- feedback: float32 [32, 2, 256, 3072], P('section', None, None, 'tensor'), may hold values from -4 to 4
- basis: float32 [3072, 128], P('tensor'), may hold values from -0.3125 to 0.3125
Outputs:
- grad_out_weight: bfloat16 [32, 2048, 3072], P('section', 'tensor')
- grad_value_weight: bfloat16 [32, 3072, 2048], P('section', None, 'tensor')
- new_feedback: float32 [32, 2, 256, 3072], P('section', None, None, 'tensor')
- rebuilt: bfloat16 [32, 2, 256, 3072], P('section', None, None, 'tensor')
The draws below stay inside these ranges and needn't reach their ends.
Inputs may be any that keep to these rules, and one draw needn't show every extreme that they name: `scores`: only entries with key position at or before the query position are read.
All inputs are finite; a program needn't handle non-finite values.
Results may differ from the reference program's by a relative error of at most 0.015.
Values may be sent and summed in bfloat16 or wider, within the bound.
A program may use at most 64 MiB of HBM per device.

```python
from functools import partial
import jax
import jax.numpy as jnp
from jax import lax

D = 3072
HEADS = 16
HEAD = 128
RANK = 128
TOK = 256
MICRO = 2
HD = 2048
SHARD = 384
N_SECTION = 32
N_TENSOR = 8


def draw_scores(key, part):
    key = jax.random.fold_in(key, 7)
    key_base = jax.random.fold_in(key, 0)
    shape = (N_SECTION, MICRO, HEADS, TOK, TOK)
    result = jnp.clip(2.0 * jax.random.normal(key_base, shape, jnp.float32), -12.0, 12.0)
    return result.astype(jnp.bfloat16)


def block_levels(key, shape, cuts, least, top_value):
    gain = 1.0
    for dim, parts in cuts:
        draws = jax.random.uniform(jax.random.fold_in(jax.random.fold_in(key, 6), dim), (parts,), jnp.float32, least / len(cuts), top_value / len(cuts))
        gain = gain * jnp.repeat(jnp.exp(draws), shape[dim] // parts).reshape((-1,) + (1,) * (len(shape) - 1 - dim))
    return gain


def bell_draw(stream_key, dims, deviation, most, cuts=(), held_as=jnp.bfloat16):
    level = block_levels(stream_key, dims, cuts, -0.22, 0.18) if cuts else 1.0
    values = jax.random.normal(stream_key, dims, jnp.float32) * deviation * level
    return jnp.minimum(jnp.maximum(values, -most), most).astype(held_as)


def setup_inputs(seed: int = 0) -> dict:
    streams_of = jax.random.split(jax.random.key(seed), 8)
    layer_input = bell_draw(streams_of[0], (N_SECTION, MICRO, TOK, D), 1.0, 6.0, ((0, 32), (3, 8)))
    upstream = bell_draw(streams_of[1], (N_SECTION, MICRO, TOK, D), 1.0, 6.0, ((0, 32), (3, 8)))
    scores = draw_scores(jax.random.fold_in(streams_of[7], 71), 0)
    value_weight = bell_draw(streams_of[3], (N_SECTION, D, HD), D ** -0.5, 0.109375, ((0, 32), (2, 8)))
    out_weight = bell_draw(streams_of[4], (N_SECTION, HD, D), HD ** -0.5, 0.125, ((0, 32), (1, 8)))
    feedback = bell_draw(streams_of[5], (N_SECTION, MICRO, TOK, D), 0.5, 4.0, ((0, 32), (3, 8)), jnp.float32)
    basis = bell_draw(streams_of[6], (D, RANK), SHARD ** -0.5, 0.3125, ((0, 8),), jnp.float32)
    return dict(layer_input=layer_input, upstream=upstream, scores=scores, value_weight=value_weight, out_weight=out_weight, feedback=feedback, basis=basis)


def causal_probs(raw_scores):
    length = raw_scores.shape[-1]
    row_ids = lax.broadcasted_iota(jnp.int32, (length, length), 0)
    col_ids = lax.broadcasted_iota(jnp.int32, (length, length), 1)
    causal = col_ids <= row_ids
    raised = jnp.where(causal, raw_scores.astype(jnp.float32), -1e30)
    largest = jnp.max(raised, axis=-1, keepdims=True)
    powers = jnp.where(causal, jnp.exp(raised - largest), 0.0)
    return (powers / jnp.sum(powers, axis=-1, keepdims=True)).astype(jnp.bfloat16)


def section_backward(pieces, basis):
    layer_input, upstream, scores, value_weight, out_weight, feedback = pieces
    row_count = MICRO * TOK
    flat_x = layer_input.reshape(row_count, D)
    flat_grad = upstream.reshape(row_count, D)
    value_act = jnp.dot(flat_x, value_weight, preferred_element_type=jnp.float32).astype(jnp.bfloat16)
    value_act = value_act.reshape(MICRO, TOK, HEADS, HEAD)
    attention = causal_probs(scores)
    attended = jnp.einsum("bhqk,bkhd->bqhd", attention.astype(jnp.float32), value_act.astype(jnp.float32))
    attended = attended.astype(jnp.bfloat16).reshape(row_count, HD)
    attended_grad = jnp.dot(flat_grad, out_weight.T, preferred_element_type=jnp.float32).astype(jnp.bfloat16)
    grad_out_weight = jnp.dot(attended.T, flat_grad, preferred_element_type=jnp.float32).astype(jnp.bfloat16)
    value_grad = jnp.einsum("bhqk,bqhd->bkhd", attention.astype(jnp.float32),
                            attended_grad.reshape(MICRO, TOK, HEADS, HEAD).astype(jnp.float32))
    value_grad = value_grad.astype(jnp.bfloat16).reshape(row_count, HD)
    grad_value_weight = jnp.dot(flat_x.T, value_grad, preferred_element_type=jnp.float32).astype(jnp.bfloat16)
    total = flat_grad.astype(jnp.float32) + jnp.dot(value_grad, value_weight.T, preferred_element_type=jnp.float32)
    carried = total + feedback.reshape(row_count, D)
    blocks = carried.reshape(row_count, N_TENSOR, SHARD).transpose(1, 0, 2)
    basis_blocks = basis.reshape(N_TENSOR, SHARD, RANK)
    factors = jnp.einsum("nrs,nsk->nrk", blocks, basis_blocks, precision=lax.Precision.HIGHEST).astype(jnp.bfloat16)
    approx = jnp.einsum("nrk,nsk->nrs", factors.astype(jnp.float32), basis_blocks, precision=lax.Precision.HIGHEST)
    new_feedback = (blocks - approx).transpose(1, 0, 2).reshape(MICRO, TOK, D)
    return grad_out_weight, grad_value_weight, new_feedback, factors


def reference(layer_input, upstream, scores, value_weight, out_weight, feedback, basis):
    grad_out_weight, grad_value_weight, new_feedback, factors = lax.map(
        partial(section_backward, basis=basis),
        (layer_input, upstream, scores, value_weight, out_weight, feedback))
    following = jnp.concatenate([factors[1:], jnp.zeros_like(factors[:1])], axis=0)
    basis_blocks = basis.reshape(N_TENSOR, SHARD, RANK)
    rebuilt = jnp.einsum("snrk,nck->snrc", following.astype(jnp.float32), basis_blocks,
                         precision=lax.Precision.HIGHEST)
    rebuilt = rebuilt.transpose(0, 2, 1, 3).reshape(N_SECTION, MICRO, TOK, D).astype(jnp.bfloat16)
    return grad_out_weight, grad_value_weight, new_feedback, rebuilt
```

```python
import functools

import jax
import jax.numpy as jnp
from jax import lax
from jax.experimental import pallas as pl
from jax.experimental.pallas import tpu as pltpu
from jax.sharding import PartitionSpec as P

MESH = pl.DeviceIdType.MESH
NT = (((1,), (1,)), ((), ()))
TN = (((0,), (0,)), ((), ()))
F32 = jnp.float32
BF16 = jnp.bfloat16


def dot(a, b, dims=(((1,), (0,)), ((), ()))):
    return lax.dot_general(a, b, dims, preferred_element_type=F32)


def halves(value):
    high = value.astype(BF16)
    return high, (value - high.astype(F32)).astype(BF16)


def body(
    micro, heads, n_section,
    x_hbm, u_hbm, scores_hbm, wv_hbm, wo_hbm, feedback_hbm, basis_hbm,
    gow_hbm, gvw_hbm, new_hbm, rebuilt_hbm,
    u, x, wv, wo, wv_far, scores, feedback, basis,
    att, att_t, sums, vg, vg_far, parts, out_stage, in_hop, in_left, in_right,
    factors, factors_in, gow, gvw, new, rebuilt,
    load_sem, send_sem, recv_sem, store_sem,
):
    rows, width = u_hbm.shape
    half = rows // 2
    length = rows // micro
    inner = wv_hbm.shape[1]
    head = inner // heads

    s = lax.axis_index("section")
    t = lax.axis_index("tensor")
    chip, core = t // 2, lax.rem(t, 2)

    def place(step, which):
        return lax.rem(chip + step, 4) * 2 + which

    right = (s, place(1, core))
    left = (s, place(3, core))
    sister = (s, place(0, 1 - core))
    behind = (lax.rem(s + n_section - 1, n_section), t)
    ahead = (lax.rem(s + 1, n_section), t)

    owner = [place(step, which) for which in (core, 1 - core) for step in (0, 3, 1, 2)]

    def block_of(slot):
        return pl.ds(pl.multiple_of(owner[slot] * width, 128), width)

    lo, hi = pl.ds(0, half), pl.ds(half, half)

    loads = []

    def load(src, dst):
        copy = pltpu.make_async_copy(src, dst, load_sem.at[len(loads)])
        copy.start()
        loads.append(copy)
        return copy

    got_scores = load(scores_hbm, scores)
    got_u = load(u_hbm, u.at[0])
    got_wo = load(wo_hbm, wo)
    got_wv = load(wv_hbm, wv)
    got_x = load(x_hbm, x.at[0])
    got_feedback = load(feedback_hbm, feedback)
    got_basis = load(basis_hbm, basis)

    barrier = pltpu.get_barrier_semaphore()
    peers = (right, left, sister, behind, ahead)
    for peer in peers:
        pl.semaphore_signal(barrier, inc=1, device_id=peer, device_id_type=MESH)
    pl.semaphore_wait(barrier, len(peers))

    sent = []

    def send(src, dst, device):
        i = len(sent)
        copy = pltpu.make_async_remote_copy(
            src_ref=src, dst_ref=dst, send_sem=send_sem.at[i], recv_sem=recv_sem.at[i],
            device_id=device, device_id_type=MESH,
        )
        copy.start()
        sent.append(copy)
        return copy

    u1lo = send(u_hbm.at[lo], u.at[1, lo], right)
    u2hi = send(u_hbm.at[hi], u.at[2, hi], left)
    u1hi = send(u_hbm.at[hi], u.at[1, hi], right)
    u2lo = send(u_hbm.at[lo], u.at[2, lo], left)
    u4 = send(u_hbm, u.at[4], sister)
    far = []
    for step in range(4):
        block = pl.ds(pl.multiple_of(place(step, 1 - core) * width, 128), width)
        far.append(send(wv_hbm.at[block], wv_far.at[step], sister))

    got_scores.wait()
    query = lax.broadcasted_iota(jnp.int32, (length, length), 0)
    key = lax.broadcasted_iota(jnp.int32, (length, length), 1)
    causal = key <= query
    for i in range(micro * heads):
        raised = jnp.where(causal, scores[i].astype(F32), -1e30)
        largest = jnp.max(raised, axis=-1, keepdims=True)
        powers = jnp.where(causal, jnp.exp(raised - largest), 0.0)
        probs = powers / jnp.sum(powers, axis=-1, keepdims=True)
        att[i] = probs.astype(BF16)
        att_t[i] = probs.T.astype(BF16)

    def add_u(slot, first=False):
        term = dot(u[slot], wo[:, block_of(slot)], NT)
        sums[...] = term if first else sums[...] + term

    got_u.wait()
    got_wo.wait()
    add_u(0, True)

    u1lo.wait_recv()
    u3lo = send(u.at[1, lo], u.at[3, lo], right)
    u5lo = send(u.at[1, lo], u.at[5, lo], sister)
    u2hi.wait_recv()
    u3hi = send(u.at[2, hi], u.at[3, hi], left)
    u6hi = send(u.at[2, hi], u.at[6, hi], sister)
    u4.wait_recv()
    add_u(4)
    u1hi.wait_recv()
    u5hi = send(u.at[1, hi], u.at[5, hi], sister)
    u2lo.wait_recv()
    u6lo = send(u.at[2, lo], u.at[6, lo], sister)

    x1lo = send(x_hbm.at[lo], x.at[1, lo], right)
    x2hi = send(x_hbm.at[hi], x.at[2, hi], left)
    x4 = send(x_hbm, x.at[4], sister)

    add_u(1)
    add_u(2)
    u5lo.wait_recv()
    u5hi.wait_recv()
    add_u(5)
    u6lo.wait_recv()
    u6hi.wait_recv()
    add_u(6)
    u3lo.wait_recv()
    u7lo = send(u.at[3, lo], u.at[7, lo], sister)
    u3hi.wait_recv()
    u7hi = send(u.at[3, hi], u.at[7, hi], sister)
    add_u(3)
    u7lo.wait_recv()
    u7hi.wait_recv()
    add_u(7)

    x1hi = send(x_hbm.at[hi], x.at[1, hi], right)
    x2lo = send(x_hbm.at[lo], x.at[2, lo], left)

    for b in range(micro):
        for h in range(heads):
            at_rows, at_columns = pl.ds(b * length, length), pl.ds(h * head, head)
            grad = dot(att_t[b * heads + h], sums[at_rows, at_columns].astype(BF16))
            vg[at_rows, at_columns] = grad.astype(BF16)
    vg_copy = send(vg, vg_far, sister)

    got_wv.wait()

    def partial(step):
        block = pl.ds(pl.multiple_of(place(step, core) * width, 128), width)
        near = dot(vg[...], wv[block, :], NT)
        return near, wv_far.at[step]

    near, _ = partial(2)
    parts[2] = near
    for copy in far:
        copy.wait_recv()
    vg_copy.wait_recv()
    out_stage[0] = (parts[2] + dot(vg_far[...], wv_far[2], NT)).astype(BF16).reshape(2, half, width)
    hop_right = send(out_stage.at[0, 0], in_hop.at[0], right)
    hop_left = send(out_stage.at[0, 1], in_hop.at[1], left)
    for step in (1, 3, 0):
        near, weight = partial(step)
        parts[step] = near + dot(vg_far[...], weight[...], NT)
        if step == 1:
            out_stage[1, 1] = parts[1, half:].astype(BF16)
            last_right_hi = send(out_stage.at[1, 1], in_left.at[1], right)
        if step == 3:
            out_stage[2, 0] = parts[3, :half].astype(BF16)
            last_left_lo = send(out_stage.at[2, 0], in_right.at[0], left)

    def add_x(slot, first=False):
        term = dot(x[slot], wv[block_of(slot), :])
        sums[...] = term if first else sums[...] + term

    stores = []

    def store(src, dst):
        copy = pltpu.make_async_copy(src, dst, store_sem.at[len(stores)])
        copy.start()
        stores.append(copy)

    def grad_value(slot):
        gvw[slot] = dot(x[slot], vg[...], TN).astype(BF16)
        store(gvw.at[slot], gvw_hbm.at[block_of(slot)])

    def take_x(slot, first=False):
        add_x(slot, first)
        grad_value(slot)

    got_x.wait()
    take_x(0, True)

    x1lo.wait_recv()
    x3lo = send(x.at[1, lo], x.at[3, lo], right)
    x5lo = send(x.at[1, lo], x.at[5, lo], sister)
    x2hi.wait_recv()
    x3hi = send(x.at[2, hi], x.at[3, hi], left)
    x6hi = send(x.at[2, hi], x.at[6, hi], sister)

    hop_right.wait_recv()
    out_stage[1, 0] = (parts[1, :half] + in_hop[0].astype(F32)).astype(BF16)
    last_right_lo = send(out_stage.at[1, 0], in_left.at[0], right)
    hop_left.wait_recv()
    out_stage[2, 1] = (parts[3, half:] + in_hop[1].astype(F32)).astype(BF16)
    last_left_hi = send(out_stage.at[2, 1], in_right.at[1], left)

    x4.wait_recv()
    take_x(4)

    x1hi.wait_recv()
    x5hi = send(x.at[1, hi], x.at[5, hi], sister)
    x2lo.wait_recv()
    x6lo = send(x.at[2, lo], x.at[6, lo], sister)
    take_x(1)
    take_x(2)
    x5lo.wait_recv()
    x5hi.wait_recv()
    take_x(5)
    x6lo.wait_recv()
    x6hi.wait_recv()
    take_x(6)

    got_feedback.wait()
    got_basis.wait()
    basis_high, basis_low = halves(basis[...])
    feedback[...] += u[0].astype(F32) + parts[0]
    last_right_lo.wait_recv()
    last_right_hi.wait_recv()
    last_left_lo.wait_recv()
    last_left_hi.wait_recv()
    carried = feedback[...] + in_left[...].astype(F32).reshape(rows, width)
    carried = carried + in_right[...].astype(F32).reshape(rows, width)
    high, low = halves(carried)
    factors[...] = (dot(high, basis_high) + dot(low, basis_high) + dot(high, basis_low)).astype(BF16)
    factor_copy = send(factors, factors_in, behind)
    own = factors[...]
    new[...] = carried - (dot(own, basis_high, NT) + dot(own, basis_low, NT))
    store(new, new_hbm)

    x3lo.wait_recv()
    x7lo = send(x.at[3, lo], x.at[7, lo], sister)
    x3hi.wait_recv()
    x7hi = send(x.at[3, hi], x.at[7, hi], sister)
    take_x(3)

    factor_copy.wait_recv()
    arrived = factors_in[...]
    built = dot(arrived, basis_high, NT) + dot(arrived, basis_low, NT)
    rebuilt[...] = jnp.where(s == n_section - 1, 0.0, built).astype(BF16)
    store(rebuilt, rebuilt_hbm)

    x7lo.wait_recv()
    x7hi.wait_recv()
    take_x(7)

    for b in range(micro):
        for h in range(heads):
            at_rows, at_columns = pl.ds(b * length, length), pl.ds(h * head, head)
            value = dot(att[b * heads + h], sums[at_rows, at_columns].astype(BF16))
            vg_far[at_rows, at_columns] = value.astype(BF16)
    attended = vg_far[...]
    for slot in range(8):
        gow[slot] = dot(attended, u[slot], TN).astype(BF16)
        store(gow.at[slot], gow_hbm.at[:, block_of(slot)])

    for copy in stores:
        copy.wait()
    for copy in sent:
        copy.wait_send()


def on_device(n_section, layer_input, upstream, scores, value_weight, out_weight, feedback, basis):
    _, micro, length, width = layer_input.shape
    rows, half = micro * length, micro * length // 2
    heads = scores.shape[2]
    model, inner = value_weight.shape[1:]
    rank = basis.shape[1]
    vmem = pltpu.VMEM
    anywhere = pl.BlockSpec(memory_space=pl.ANY)
    gow, gvw, new, rebuilt = pl.pallas_call(
        functools.partial(body, micro, heads, n_section),
        out_shape=(
            jax.ShapeDtypeStruct((inner, model), BF16),
            jax.ShapeDtypeStruct((model, inner), BF16),
            jax.ShapeDtypeStruct((rows, width), F32),
            jax.ShapeDtypeStruct((rows, width), BF16),
        ),
        in_specs=[anywhere] * 7,
        out_specs=(anywhere,) * 4,
        scratch_shapes=[
            vmem((8, rows, width), BF16),
            vmem((8, rows, width), BF16),
            vmem((model, inner), BF16),
            vmem((inner, model), BF16),
            vmem((4, width, inner), BF16),
            vmem((micro * heads, length, length), BF16),
            vmem((rows, width), F32),
            vmem((width, rank), F32),
            vmem((micro * heads, length, length), BF16),
            vmem((micro * heads, length, length), BF16),
            vmem((rows, inner), F32),
            vmem((rows, inner), BF16),
            vmem((rows, inner), BF16),
            vmem((4, rows, width), F32),
            vmem((3, 2, half, width), BF16),
            vmem((2, half, width), BF16),
            vmem((2, half, width), BF16),
            vmem((2, half, width), BF16),
            vmem((rows, rank), BF16),
            vmem((rows, rank), BF16),
            vmem((8, inner, width), BF16),
            vmem((8, width, inner), BF16),
            vmem((rows, width), F32),
            vmem((rows, width), BF16),
            pltpu.SemaphoreType.DMA((7,)),
            pltpu.SemaphoreType.DMA((40,)),
            pltpu.SemaphoreType.DMA((40,)),
            pltpu.SemaphoreType.DMA((18,)),
        ],
        compiler_params=pltpu.CompilerParams(
            collective_id=0, has_side_effects=True, vmem_limit_bytes=56 << 20
        ),
    )(
        layer_input.reshape(rows, width),
        upstream.reshape(rows, width),
        scores.reshape(micro * heads, length, length),
        value_weight[0],
        out_weight[0],
        feedback.reshape(rows, width),
        basis,
    )
    shape = (1, micro, length, width)
    return gow[None], gvw[None], new.reshape(shape), rebuilt.reshape(shape)


def solution(mesh):
    in_specs = (
        P("section", None, None, "tensor"),
        P("section", None, None, "tensor"),
        P("section", None, "tensor", None, None),
        P("section", None, "tensor"),
        P("section", "tensor", None),
        P("section", None, None, "tensor"),
        P("tensor", None),
    )
    out_specs = (
        P("section", "tensor", None),
        P("section", None, "tensor"),
        P("section", None, None, "tensor"),
        P("section", None, None, "tensor"),
    )
    return jax.shard_map(
        functools.partial(on_device, mesh.shape["section"]),
        mesh=mesh, in_specs=in_specs, out_specs=out_specs, check_vma=False,
    )
```

```python
import functools

import jax
import jax.numpy as jnp
from jax import lax
from jax.experimental import pallas as pl
from jax.experimental.pallas import tpu as pltpu
from jax.sharding import PartitionSpec as P

MESH = pl.DeviceIdType.MESH
NT = (((1,), (1,)), ((), ()))
TN = (((0,), (0,)), ((), ()))
F32 = jnp.float32
BF16 = jnp.bfloat16


def dot(a, b, dims=(((1,), (0,)), ((), ()))):
    return lax.dot_general(a, b, dims, preferred_element_type=F32)


def halves(value):
    high = value.astype(BF16)
    return high, (value - high.astype(F32)).astype(BF16)


def blocks(chip, core, width):
    owner = [
        lax.rem(chip + step, 4) * 2 + which for which in (core, 1 - core) for step in (0, 3, 1, 2)
    ]
    return lambda slot: pl.ds(pl.multiple_of(owner[slot] * width, 128), width)


def body(
    micro, heads, n_section,
    x_hbm, u_hbm, scores_hbm, wv_hbm, wo_hbm, feedback_hbm, basis_hbm,
    u, x, wv, att, sums, vg, gvw, new, rebuilt,
    wo, wv_far, scores, feedback, basis,
    att_t, vg_far, parts, out_stage, in_hop, in_left, in_right,
    factors, factors_in,
    load_sem, send_sem, recv_sem,
):
    rows, width = u_hbm.shape
    half = rows // 2
    length = rows // micro
    inner = wv_hbm.shape[1]
    head = inner // heads

    s = lax.axis_index("section")
    t = lax.axis_index("tensor")
    chip, core = t // 2, lax.rem(t, 2)

    def place(step, which):
        return lax.rem(chip + step, 4) * 2 + which

    right = (s, place(1, core))
    left = (s, place(3, core))
    sister = (s, place(0, 1 - core))
    behind = (lax.rem(s + n_section - 1, n_section), t)
    ahead = (lax.rem(s + 1, n_section), t)

    block_of = blocks(chip, core, width)

    lo, hi = pl.ds(0, half), pl.ds(half, half)

    loads = []

    def load(src, dst):
        copy = pltpu.make_async_copy(src, dst, load_sem.at[len(loads)])
        copy.start()
        loads.append(copy)
        return copy

    got_scores = load(scores_hbm, scores)
    got_u = load(u_hbm, u.at[0])
    got_wo = load(wo_hbm, wo)
    got_wv = load(wv_hbm, wv)
    got_x = load(x_hbm, x.at[0])
    got_feedback = load(feedback_hbm, feedback)
    got_basis = load(basis_hbm, basis)

    barrier = pltpu.get_barrier_semaphore()
    peers = (right, left, sister, behind, ahead)
    for peer in peers:
        pl.semaphore_signal(barrier, inc=1, device_id=peer, device_id_type=MESH)
    pl.semaphore_wait(barrier, len(peers))

    sent = []

    def send(src, dst, device):
        i = len(sent)
        copy = pltpu.make_async_remote_copy(
            src_ref=src, dst_ref=dst, send_sem=send_sem.at[i], recv_sem=recv_sem.at[i],
            device_id=device, device_id_type=MESH,
        )
        copy.start()
        sent.append(copy)
        return copy

    u1lo = send(u_hbm.at[lo], u.at[1, lo], right)
    u2hi = send(u_hbm.at[hi], u.at[2, hi], left)
    u1hi = send(u_hbm.at[hi], u.at[1, hi], right)
    u2lo = send(u_hbm.at[lo], u.at[2, lo], left)
    u4 = send(u_hbm, u.at[4], sister)
    far = []
    for step in range(4):
        block = pl.ds(pl.multiple_of(place(step, 1 - core) * width, 128), width)
        far.append(send(wv_hbm.at[block], wv_far.at[step], sister))

    got_scores.wait()
    query = lax.broadcasted_iota(jnp.int32, (length, length), 0)
    key = lax.broadcasted_iota(jnp.int32, (length, length), 1)
    causal = key <= query
    for i in range(micro * heads):
        raised = jnp.where(causal, scores[i].astype(F32), -1e30)
        largest = jnp.max(raised, axis=-1, keepdims=True)
        powers = jnp.where(causal, jnp.exp(raised - largest), 0.0)
        probs = powers / jnp.sum(powers, axis=-1, keepdims=True)
        att[i] = probs.astype(BF16)
        att_t[i] = probs.T.astype(BF16)

    def add_u(slot, first=False):
        term = dot(u[slot], wo[:, block_of(slot)], NT)
        sums[...] = term if first else sums[...] + term

    got_u.wait()
    got_wo.wait()
    add_u(0, True)

    u1lo.wait_recv()
    u3lo = send(u.at[1, lo], u.at[3, lo], right)
    u5lo = send(u.at[1, lo], u.at[5, lo], sister)
    u2hi.wait_recv()
    u3hi = send(u.at[2, hi], u.at[3, hi], left)
    u6hi = send(u.at[2, hi], u.at[6, hi], sister)
    u4.wait_recv()
    add_u(4)
    u1hi.wait_recv()
    u5hi = send(u.at[1, hi], u.at[5, hi], sister)
    u2lo.wait_recv()
    u6lo = send(u.at[2, lo], u.at[6, lo], sister)

    add_u(1)
    add_u(2)
    u5lo.wait_recv()
    u5hi.wait_recv()
    add_u(5)
    u6lo.wait_recv()
    u6hi.wait_recv()
    add_u(6)
    x1lo = send(x_hbm.at[lo], x.at[1, lo], right)
    x2hi = send(x_hbm.at[hi], x.at[2, hi], left)
    x4 = send(x_hbm, x.at[4], sister)
    u3lo.wait_recv()
    u7lo = send(u.at[3, lo], u.at[7, lo], sister)
    u3hi.wait_recv()
    u7hi = send(u.at[3, hi], u.at[7, hi], sister)
    add_u(3)
    u7lo.wait_recv()
    u7hi.wait_recv()
    add_u(7)

    for b in range(micro):
        for h in range(heads):
            at_rows, at_columns = pl.ds(b * length, length), pl.ds(h * head, head)
            grad = dot(att_t[b * heads + h], sums[at_rows, at_columns].astype(BF16))
            vg[at_rows, at_columns] = grad.astype(BF16)
    vg_copy = send(vg, vg_far, sister)

    got_wv.wait()

    def partial(step):
        block = pl.ds(pl.multiple_of(place(step, core) * width, 128), width)
        near = dot(vg[...], wv[block, :], NT)
        return near, wv_far.at[step]

    near, _ = partial(2)
    parts[2] = near
    for copy in far:
        copy.wait_recv()
    vg_copy.wait_recv()
    out_stage[0] = (parts[2] + dot(vg_far[...], wv_far[2], NT)).astype(BF16).reshape(2, half, width)
    hop_right = send(out_stage.at[0, 0], in_hop.at[0], right)
    hop_left = send(out_stage.at[0, 1], in_hop.at[1], left)
    for step in (1, 3, 0):
        near, weight = partial(step)
        parts[step] = near + dot(vg_far[...], weight[...], NT)
        if step == 1:
            out_stage[1, 1] = parts[1, half:].astype(BF16)
            last_right_hi = send(out_stage.at[1, 1], in_left.at[1], right)
        if step == 3:
            out_stage[2, 0] = parts[3, :half].astype(BF16)
            last_left_lo = send(out_stage.at[2, 0], in_right.at[0], left)

    def add_x(slot, first=False):
        term = dot(x[slot], wv[block_of(slot), :])
        sums[...] = term if first else sums[...] + term

    def grad_value(slot):
        gvw[slot] = dot(x[slot], vg[...], TN).astype(BF16)

    def take_x(slot, first=False):
        add_x(slot, first)
        grad_value(slot)

    got_x.wait()
    take_x(0, True)
    x4.wait_recv()
    take_x(4)

    x1lo.wait_recv()
    x5lo = send(x.at[1, lo], x.at[5, lo], sister)
    x2hi.wait_recv()
    x6hi = send(x.at[2, hi], x.at[6, hi], sister)

    hop_right.wait_recv()
    out_stage[1, 0] = (parts[1, :half] + in_hop[0].astype(F32)).astype(BF16)
    last_right_lo = send(out_stage.at[1, 0], in_left.at[0], right)
    hop_left.wait_recv()
    out_stage[2, 1] = (parts[3, half:] + in_hop[1].astype(F32)).astype(BF16)
    last_left_hi = send(out_stage.at[2, 1], in_right.at[1], left)

    x1hi = send(x_hbm.at[hi], x.at[1, hi], right)
    x2lo = send(x_hbm.at[lo], x.at[2, lo], left)
    x3lo = send(x.at[1, lo], x.at[3, lo], right)
    x3hi = send(x.at[2, hi], x.at[3, hi], left)

    got_feedback.wait()
    got_basis.wait()
    basis_high, basis_low = halves(basis[...])
    feedback[...] += u[0].astype(F32) + parts[0]
    last_right_hi.wait_recv()
    last_left_lo.wait_recv()
    last_right_lo.wait_recv()
    last_left_hi.wait_recv()
    carried = feedback[...] + in_left[...].astype(F32).reshape(rows, width)
    carried = carried + in_right[...].astype(F32).reshape(rows, width)
    high, low = halves(carried)
    factors[...] = (dot(high, basis_high) + dot(low, basis_high) + dot(high, basis_low)).astype(BF16)
    factor_copy = send(factors, factors_in, behind)
    own = factors[...]
    new[...] = carried - (dot(own, basis_high, NT) + dot(own, basis_low, NT))

    x1hi.wait_recv()
    x5hi = send(x.at[1, hi], x.at[5, hi], sister)
    x2lo.wait_recv()
    x6lo = send(x.at[2, lo], x.at[6, lo], sister)
    take_x(1)
    take_x(2)

    factor_copy.wait_recv()
    arrived = factors_in[...]
    built = dot(arrived, basis_high, NT) + dot(arrived, basis_low, NT)
    rebuilt[...] = jnp.where(s == n_section - 1, 0.0, built).astype(BF16)

    x5lo.wait_recv()
    x5hi.wait_recv()
    take_x(5)
    x6lo.wait_recv()
    x6hi.wait_recv()
    take_x(6)

    x3lo.wait_recv()
    x7lo = send(x.at[3, lo], x.at[7, lo], sister)
    x3hi.wait_recv()
    x7hi = send(x.at[3, hi], x.at[7, hi], sister)
    take_x(3)
    x7lo.wait_recv()
    x7hi.wait_recv()
    for copy in sent:
        copy.wait_send()


def finish(
    micro, heads, u, x, wv, att, sums, vg, gvw, new, rebuilt,
    gow_hbm, gvw_hbm, new_hbm, rebuilt_hbm, last, gow, attended, store_sem,
):
    width = u.shape[2]
    length = att.shape[1]
    head = wv.shape[1] // heads
    t = lax.axis_index("tensor")
    block_of = blocks(t // 2, lax.rem(t, 2), width)
    stores = []

    def store(src, dst):
        copy = pltpu.make_async_copy(src, dst, store_sem.at[len(stores)])
        copy.start()
        stores.append(copy)

    for slot in range(7):
        store(gvw.at[slot], gvw_hbm.at[block_of(slot)])
    store(new, new_hbm)
    store(rebuilt, rebuilt_hbm)

    value = sums[...] + dot(x[7], wv[block_of(7), :])
    for b in range(micro):
        for h in range(heads):
            at_rows, at_columns = slice(b * length, (b + 1) * length), slice(h * head, (h + 1) * head)
            mixed = dot(att[b * heads + h], value[at_rows, at_columns].astype(BF16))
            attended[at_rows, at_columns] = mixed.astype(BF16)
    for slot in range(8):
        gow[slot] = dot(attended[...], u[slot], TN).astype(BF16)
        store(gow.at[slot], gow_hbm.at[:, block_of(slot)])
    last[...] = dot(x[7], vg[...], TN).astype(BF16)
    store(last, gvw_hbm.at[block_of(7)])
    for copy in stores:
        copy.wait()


def on_device(n_section, layer_input, upstream, scores, value_weight, out_weight, feedback, basis):
    _, micro, length, width = layer_input.shape
    rows, half = micro * length, micro * length // 2
    heads = scores.shape[2]
    model, inner = value_weight.shape[1:]
    rank = basis.shape[1]
    vmem = pltpu.VMEM
    anywhere = pl.BlockSpec(memory_space=pl.ANY)
    whole = pl.BlockSpec(memory_space=vmem)
    held = pl.pallas_call(
        functools.partial(body, micro, heads, n_section),
        out_shape=(
            vmem((8, rows, width), BF16),
            vmem((8, rows, width), BF16),
            vmem((model, inner), BF16),
            vmem((micro * heads, length, length), BF16),
            vmem((rows, inner), F32),
            vmem((rows, inner), BF16),
            vmem((8, width, inner), BF16),
            vmem((rows, width), F32),
            vmem((rows, width), BF16),
        ),
        in_specs=[anywhere] * 7,
        out_specs=(whole,) * 9,
        scratch_shapes=[
            vmem((inner, model), BF16),
            vmem((4, width, inner), BF16),
            vmem((micro * heads, length, length), BF16),
            vmem((rows, width), F32),
            vmem((width, rank), F32),
            vmem((micro * heads, length, length), BF16),
            vmem((rows, inner), BF16),
            vmem((4, rows, width), F32),
            vmem((3, 2, half, width), BF16),
            vmem((2, half, width), BF16),
            vmem((2, half, width), BF16),
            vmem((2, half, width), BF16),
            vmem((rows, rank), BF16),
            vmem((rows, rank), BF16),
            pltpu.SemaphoreType.DMA((7,)),
            pltpu.SemaphoreType.DMA((40,)),
            pltpu.SemaphoreType.DMA((40,)),
        ],
        compiler_params=pltpu.CompilerParams(
            collective_id=0, has_side_effects=True, vmem_limit_bytes=40 << 20
        ),
    )(*(
        pltpu.with_memory_space_constraint(value, pltpu.HBM)
        for value in (
            layer_input.reshape(rows, width),
            upstream.reshape(rows, width),
            scores.reshape(micro * heads, length, length),
            value_weight[0],
            out_weight[0],
            feedback.reshape(rows, width),
            basis,
        )
    ))
    u, x, *others = held
    gow, gvw, new, rebuilt = pl.pallas_call(
        functools.partial(finish, micro, heads),
        out_shape=(
            jax.ShapeDtypeStruct((inner, model), BF16),
            jax.ShapeDtypeStruct((model, inner), BF16),
            jax.ShapeDtypeStruct((rows, width), F32),
            jax.ShapeDtypeStruct((rows, width), BF16),
        ),
        in_specs=[whole] * 9,
        out_specs=(anywhere,) * 4,
        scratch_shapes=[
            vmem((width, inner), BF16),
            vmem((8, inner, width), BF16),
            vmem((rows, inner), BF16),
            pltpu.SemaphoreType.DMA((18,)),
        ],
        compiler_params=pltpu.CompilerParams(vmem_limit_bytes=16 << 20),
    )(*(pltpu.with_memory_space_constraint(value, pltpu.VMEM) for value in (u, x, *others)))
    shape = (1, micro, length, width)
    return gow[None], gvw[None], new.reshape(shape), rebuilt.reshape(shape)


def solution(mesh):
    in_specs = (
        P("section", None, None, "tensor"),
        P("section", None, None, "tensor"),
        P("section", None, "tensor", None, None),
        P("section", None, "tensor"),
        P("section", "tensor", None),
        P("section", None, None, "tensor"),
        P("tensor", None),
    )
    out_specs = (
        P("section", "tensor", None),
        P("section", None, "tensor"),
        P("section", None, None, "tensor"),
        P("section", None, None, "tensor"),
    )
    return jax.shard_map(
        functools.partial(on_device, mesh.shape["section"]),
        mesh=mesh, in_specs=in_specs, out_specs=out_specs, check_vma=False,
    )
```

```python
import functools

import jax
import jax.numpy as jnp
from jax import lax
from jax.experimental import pallas as pl
from jax.experimental.pallas import tpu as pltpu
from jax.sharding import PartitionSpec as P

MESH = pl.DeviceIdType.MESH
NT = (((1,), (1,)), ((), ()))
TN = (((0,), (0,)), ((), ()))
ROW = 8
F32 = jnp.float32
BF16 = jnp.bfloat16


def dot(a, b, dims=(((1,), (0,)), ((), ()))):
    return lax.dot_general(a, b, dims, preferred_element_type=F32)


def halves(value):
    high = value.astype(BF16)
    return high, (value - high.astype(F32)).astype(BF16)


def blocks(chip, core, width):
    owner = [
        lax.rem(chip + step, 4) * 2 + which for which in (core, 1 - core) for step in (0, 3, 1, 2)
    ]
    return lambda slot: pl.ds(pl.multiple_of(owner[slot] * width, 128), width)


def body(
    micro, heads, n_section,
    x_hbm, u_hbm, scores_hbm, wv_hbm, wo_hbm, feedback_hbm, basis_hbm,
    u, x, wv, att, va, vg, gow_first, gvw, new, factors_in, basis,
    wo, wv_far, scores, feedback,
    att_t, ag, vg_far, parts, out_stage, in_hop, in_left, in_right, factors,
    load_sem, send_sem, recv_sem, factor_sem,
):
    rows, width = u_hbm.shape
    length = rows // micro
    quarter = length // 2
    inner = wv_hbm.shape[1]
    head = inner // heads

    s = lax.axis_index("section")
    t = lax.axis_index("tensor")
    chip, core = t // 2, lax.rem(t, 2)

    def place(step, which):
        return lax.rem(chip + step, 4) * 2 + which

    right = (s, place(1, core))
    left = (s, place(3, core))
    sister = (s, place(0, 1 - core))

    row_first, row_last = lax.rem(s, ROW) == 0, lax.rem(s, ROW) == ROW - 1

    def section(step):
        return lax.rem(s + n_section + step, n_section)

    behind = (jnp.where(row_first, section(ROW - 1), section(-1)), t)
    beyond = (section(-ROW), t)
    block_of = blocks(chip, core, width)

    def batch(m):
        return pl.ds(m * length, length)

    def first(m):
        return pl.ds(m * length, quarter)

    def second(m):
        return pl.ds(m * length + quarter, quarter)

    loads = []

    def load(src, dst):
        copy = pltpu.make_async_copy(src, dst, load_sem.at[len(loads)])
        copy.start()
        loads.append(copy)
        return copy

    got_scores = load(scores_hbm, scores)
    got_u = load(u_hbm, u.at[0])
    got_wo = load(wo_hbm, wo)
    got_wv = load(wv_hbm, wv)
    got_x = load(x_hbm, x.at[0])
    got_feedback = load(feedback_hbm, feedback)
    got_basis = load(basis_hbm, basis)

    barrier = pltpu.get_barrier_semaphore()
    peers = (right, left, sister, (jnp.where(row_last, section(ROW), section(1)), t))
    for peer in peers:
        pl.semaphore_signal(barrier, inc=1, device_id=peer, device_id_type=MESH)

    @pl.when(row_last)
    def _():
        pl.semaphore_signal(barrier, inc=1, device_id=(section(1 - ROW), t), device_id_type=MESH)

    pl.semaphore_wait(barrier, len(peers) + row_last.astype(jnp.int32))

    sent = []

    def send(src, dst, device):
        i = len(sent)
        copy = pltpu.make_async_remote_copy(
            src_ref=src, dst_ref=dst, send_sem=send_sem.at[i], recv_sem=recv_sem.at[i],
            device_id=device, device_id_type=MESH,
        )
        copy.start()
        sent.append(copy)
        return copy

    def arrive(*copies):
        for copy in copies:
            copy.wait_recv()

    def spread(src, dst, m):
        return (
            send(src.at[first(m)], dst.at[1, first(m)], right),
            send(src.at[second(m)], dst.at[2, second(m)], left),
            send(src.at[second(m)], dst.at[1, second(m)], right),
            send(src.at[first(m)], dst.at[2, first(m)], left),
        )

    def relay(dst, m, copies):
        arrive(copies[0])
        onward = send(dst.at[1, first(m)], dst.at[3, first(m)], right)
        arrive(copies[1])
        return onward, send(dst.at[2, second(m)], dst.at[3, second(m)], left)

    def share(dst, slot, rows_):
        return send(dst.at[slot, rows_], dst.at[slot + 4, rows_], sister)

    u_out = [spread(u_hbm, u, 0)]
    u_own = send(u_hbm, u.at[4], sister)
    far = []
    for step in range(4):
        block = pl.ds(pl.multiple_of(place(step, 1 - core) * width, 128), width)
        far.append(send(wv_hbm.at[block], wv_far.at[step], sister))

    got_scores.wait()
    query = lax.broadcasted_iota(jnp.int32, (length, length), 0)
    key = lax.broadcasted_iota(jnp.int32, (length, length), 1)
    causal = key <= query
    for i in range(micro * heads):
        raised = jnp.where(causal, scores[i].astype(F32), -1e30)
        largest = jnp.max(raised, axis=-1, keepdims=True)
        powers = jnp.where(causal, jnp.exp(raised - largest), 0.0)
        probs = powers / jnp.sum(powers, axis=-1, keepdims=True)
        att[i] = probs.astype(BF16)
        att_t[i] = probs.T.astype(BF16)

    def add_u(m, *slots):
        total = ag[batch(m)]
        for slot in slots:
            total = total + dot(u[slot, batch(m)], wo[:, block_of(slot)], NT)
        ag[batch(m)] = total

    got_u.wait()
    got_wo.wait()
    ag[...] = dot(u[0], wo[:, block_of(0)], NT)

    def value_grad(m):
        for h in range(heads):
            columns = pl.ds(h * head, head)
            grad = dot(att_t[m * heads + h], ag[batch(m), columns].astype(BF16))
            vg[batch(m), columns] = grad.astype(BF16)
        return send(vg.at[batch(m)], vg_far.at[batch(m)], sister)

    def partial(m, step):
        block = pl.ds(pl.multiple_of(place(step, core) * width, 128), width)
        near = dot(vg[batch(m)], wv[block, :], NT)
        return near + dot(vg_far[batch(m)], wv_far[step], NT)

    def begin_sums(m):
        out_stage[0, batch(m)] = partial(m, 2).astype(BF16)
        hops = (
            send(out_stage.at[0, first(m)], in_hop.at[first(m)], right),
            send(out_stage.at[0, second(m)], in_hop.at[second(m)], left),
        )
        parts[1, batch(m)] = partial(m, 1)
        out_stage[1, second(m)] = parts[1, second(m)].astype(BF16)
        ends = [send(out_stage.at[1, second(m)], in_left.at[second(m)], right)]
        parts[2, batch(m)] = partial(m, 3)
        out_stage[2, first(m)] = parts[2, first(m)].astype(BF16)
        ends.append(send(out_stage.at[2, first(m)], in_right.at[first(m)], left))
        parts[0, batch(m)] = partial(m, 0)
        return hops, ends

    def end_sums(m, hops, ends):
        arrive(hops[0])
        out_stage[1, first(m)] = (parts[1, first(m)] + in_hop[first(m)].astype(F32)).astype(BF16)
        ends.append(send(out_stage.at[1, first(m)], in_left.at[first(m)], right))
        arrive(hops[1])
        out_stage[2, second(m)] = (parts[2, second(m)] + in_hop[second(m)].astype(F32)).astype(BF16)
        ends.append(send(out_stage.at[2, second(m)], in_right.at[second(m)], left))

    def gather_u(m, copies, onward):
        arrive(*copies[2:])
        shared = share(u, 1, batch(m)), share(u, 2, batch(m))
        add_u(m, 1, 2)
        arrive(*shared)
        add_u(m, 5, 6)
        arrive(*onward)
        shared = share(u, 3, batch(m))
        add_u(m, 3)
        arrive(shared)
        add_u(m, 7)
        return value_grad(m)

    u_on = [relay(u, 0, u_out[0])]
    u_out.append(spread(u_hbm, u, 1))
    arrive(u_own)
    ag[...] += dot(u[4], wo[:, block_of(4)], NT)
    vg_copy = gather_u(0, u_out[0], u_on[0])
    u_on.append(relay(u, 1, u_out[1]))
    got_wv.wait()
    arrive(vg_copy, *far)
    hops0, ends0 = begin_sums(0)
    x_out = [spread(x_hbm, x, 0)]
    x_own = send(x_hbm, x.at[4], sister)
    vg_copy = gather_u(1, u_out[1], u_on[1])
    end_sums(0, hops0, ends0)
    arrive(vg_copy)
    hops1, ends1 = begin_sums(1)

    def add_x(m, *slots):
        total = va[batch(m)]
        for slot in slots:
            total = total + dot(x[slot, batch(m)], wv[block_of(slot), :])
        va[batch(m)] = total

    def grad_value(slot):
        gvw[slot] = dot(x[slot], vg[...], TN).astype(BF16)

    x_on = [relay(x, 0, x_out[0])]
    got_x.wait()
    va[...] = dot(x[0], wv[block_of(0), :])
    grad_value(0)
    arrive(x_own)
    va[...] += dot(x[4], wv[block_of(4), :])
    grad_value(4)
    arrive(*x_out[0][2:])
    shared = share(x, 1, batch(0)), share(x, 2, batch(0))
    add_x(0, 1, 2)
    arrive(*shared)
    add_x(0, 5, 6)
    got_feedback.wait()
    got_basis.wait()
    basis_high, basis_low = halves(basis[...])
    slot = row_first.astype(jnp.int32)

    def compress(m, ends):
        arrive(*ends)
        carried = feedback[batch(m)] + u[0, batch(m)].astype(F32) + parts[0, batch(m)]
        carried = carried + in_left[batch(m)].astype(F32) + in_right[batch(m)].astype(F32)
        high, low = halves(carried)
        found = dot(high, basis_high) + dot(low, basis_high) + dot(high, basis_low)
        own = found.astype(BF16)
        factors[batch(m)] = own
        copy = pltpu.make_async_remote_copy(
            src_ref=factors.at[batch(m)], dst_ref=factors_in.at[slot, batch(m)],
            send_sem=factor_sem.at[0, m], recv_sem=factor_sem.at[2 + slot, m],
            device_id=behind, device_id_type=MESH,
        )
        copy.start()
        new[batch(m)] = carried - (dot(own, basis_high, NT) + dot(own, basis_low, NT))
        return copy

    def passing(m, which):
        return pltpu.make_async_remote_copy(
            src_ref=factors_in.at[1, batch(m)], dst_ref=factors_in.at[which, batch(m)],
            send_sem=factor_sem.at[1, m], recv_sem=factor_sem.at[2 + which, m],
            device_id=beyond, device_id_type=MESH,
        )

    def pass_on(m):
        @pl.when(row_last)
        def _():
            passing(m, 1).wait_recv()
            passing(m, 0).start()

    factor_copies = [compress(0, ends0)]
    end_sums(1, hops1, ends1)
    x_out.append(spread(x_hbm, x, 1))
    pass_on(0)
    factor_copies.append(compress(1, ends1))

    arrive(*x_on[0])
    shared = share(x, 3, batch(0))
    add_x(0, 3)
    arrive(shared)
    add_x(0, 7)
    x_on.append(relay(x, 1, x_out[1]))
    mixed = attended(0, heads, va, att)
    for slot in range(8):
        gow_first[slot] = dot(mixed, u[slot, batch(0)])

    arrive(*x_out[1][2:])
    shared = share(x, 1, batch(1)), share(x, 2, batch(1))
    add_x(1, 1, 2)
    grad_value(1)
    grad_value(2)
    arrive(*shared)
    add_x(1, 5, 6)
    grad_value(5)
    grad_value(6)

    pass_on(1)
    arrive(x_on[1][0])
    last = [share(x, 3, first(1))]
    arrive(x_on[1][1])
    last.append(share(x, 3, second(1)))
    add_x(1, 3)
    grad_value(3)
    arrive(*last)
    for m in range(micro):
        passing(m, 0).wait_recv()
        factor_copies[m].wait_send()

    @pl.when(row_last)
    def _():
        for m in range(micro):
            passing(m, 0).wait_send()

    for copy in sent:
        copy.wait_send()


def attended(m, heads, va, att):
    length = att.shape[1]
    head = va.shape[1] // heads
    found = []
    for h in range(heads):
        value = va[pl.ds(m * length, length), pl.ds(h * head, head)]
        found.append(dot(value.T.astype(BF16), att[m * heads + h], NT).astype(BF16))
    return jnp.concatenate(found, axis=0)


def finish(
    micro, heads, n_section, u, x, wv, att, va, vg, gow_first, gvw, new, factors_in, basis,
    gow_hbm, gvw_hbm, new_hbm, rebuilt_hbm, last, gow, total, rebuilt, store_sem,
):
    width = u.shape[2]
    length = att.shape[1]
    s = lax.axis_index("section")
    t = lax.axis_index("tensor")
    block_of = blocks(t // 2, lax.rem(t, 2), width)
    stores = []

    def store(src, dst):
        copy = pltpu.make_async_copy(src, dst, store_sem.at[len(stores)])
        copy.start()
        stores.append(copy)

    for slot in range(7):
        store(gvw.at[slot], gvw_hbm.at[block_of(slot)])
    store(new, new_hbm)

    rows = pl.ds((micro - 1) * length, length)
    total[rows] = va[rows] + dot(x[7, rows], wv[block_of(7), :])
    mixed = attended(micro - 1, heads, total, att)
    for slot in range(8):
        gow[slot] = (gow_first[slot] + dot(mixed, u[slot, rows])).astype(BF16)
        store(gow.at[slot], gow_hbm.at[:, block_of(slot)])
    basis_high, basis_low = halves(basis[...])
    arrived = factors_in[0]
    built = dot(arrived, basis_high, NT) + dot(arrived, basis_low, NT)
    rebuilt[...] = jnp.where(s == n_section - 1, 0.0, built).astype(BF16)
    store(rebuilt, rebuilt_hbm)
    last[...] = dot(x[7], vg[...], TN).astype(BF16)
    store(last, gvw_hbm.at[block_of(7)])
    for copy in stores:
        copy.wait()


def on_device(n_section, layer_input, upstream, scores, value_weight, out_weight, feedback, basis):
    _, micro, length, width = layer_input.shape
    rows = micro * length
    heads = scores.shape[2]
    model, inner = value_weight.shape[1:]
    rank = basis.shape[1]
    vmem = pltpu.VMEM
    anywhere = pl.BlockSpec(memory_space=pl.ANY)
    whole = pl.BlockSpec(memory_space=vmem)
    held = pl.pallas_call(
        functools.partial(body, micro, heads, n_section),
        out_shape=(
            vmem((8, rows, width), BF16),
            vmem((8, rows, width), BF16),
            vmem((model, inner), BF16),
            vmem((micro * heads, length, length), BF16),
            vmem((rows, inner), F32),
            vmem((rows, inner), BF16),
            vmem((8, inner, width), F32),
            vmem((8, width, inner), BF16),
            vmem((rows, width), F32),
            vmem((2, rows, rank), BF16),
            vmem((width, rank), F32),
        ),
        in_specs=[anywhere] * 7,
        out_specs=(whole,) * 11,
        scratch_shapes=[
            vmem((inner, model), BF16),
            vmem((4, width, inner), BF16),
            vmem((micro * heads, length, length), BF16),
            vmem((rows, width), F32),
            vmem((micro * heads, length, length), BF16),
            vmem((rows, inner), F32),
            vmem((rows, inner), BF16),
            vmem((3, rows, width), F32),
            vmem((3, rows, width), BF16),
            vmem((rows, width), BF16),
            vmem((rows, width), BF16),
            vmem((rows, width), BF16),
            vmem((rows, rank), BF16),
            pltpu.SemaphoreType.DMA((7,)),
            pltpu.SemaphoreType.DMA((80,)),
            pltpu.SemaphoreType.DMA((80,)),
            pltpu.SemaphoreType.DMA((4, micro)),
        ],
        compiler_params=pltpu.CompilerParams(
            collective_id=0, has_side_effects=True, vmem_limit_bytes=40 << 20
        ),
    )(*(
        pltpu.with_memory_space_constraint(value, pltpu.HBM)
        for value in (
            layer_input.reshape(rows, width),
            upstream.reshape(rows, width),
            scores.reshape(micro * heads, length, length),
            value_weight[0],
            out_weight[0],
            feedback.reshape(rows, width),
            basis,
        )
    ))
    gow, gvw, new, rebuilt = pl.pallas_call(
        functools.partial(finish, micro, heads, n_section),
        out_shape=(
            jax.ShapeDtypeStruct((inner, model), BF16),
            jax.ShapeDtypeStruct((model, inner), BF16),
            jax.ShapeDtypeStruct((rows, width), F32),
            jax.ShapeDtypeStruct((rows, width), BF16),
        ),
        in_specs=[whole] * 11,
        out_specs=(anywhere,) * 4,
        scratch_shapes=[
            vmem((width, inner), BF16),
            vmem((8, inner, width), BF16),
            vmem((rows, inner), F32),
            vmem((rows, width), BF16),
            pltpu.SemaphoreType.DMA((18,)),
        ],
        compiler_params=pltpu.CompilerParams(vmem_limit_bytes=16 << 20),
    )(*(pltpu.with_memory_space_constraint(value, pltpu.VMEM) for value in held))
    shape = (1, micro, length, width)
    return gow[None], gvw[None], new.reshape(shape), rebuilt.reshape(shape)


def solution(mesh):
    in_specs = (
        P("section", None, None, "tensor"),
        P("section", None, None, "tensor"),
        P("section", None, "tensor", None, None),
        P("section", None, "tensor"),
        P("section", "tensor", None),
        P("section", None, None, "tensor"),
        P("tensor", None),
    )
    out_specs = (
        P("section", "tensor", None),
        P("section", None, "tensor"),
        P("section", None, None, "tensor"),
        P("section", None, None, "tensor"),
    )
    return jax.shard_map(
        functools.partial(on_device, mesh.shape["section"]),
        mesh=mesh, in_specs=in_specs, out_specs=out_specs, check_vma=False,
    )
```

```python
import functools

import jax
import jax.numpy as jnp
from jax import lax
from jax.experimental import pallas as pl
from jax.experimental.pallas import tpu as pltpu
from jax.sharding import PartitionSpec as P

MESH = pl.DeviceIdType.MESH
NT = (((1,), (1,)), ((), ()))
TN = (((0,), (0,)), ((), ()))
ROW = 8
F32 = jnp.float32
BF16 = jnp.bfloat16


def dot(a, b, dims=(((1,), (0,)), ((), ()))):
    return lax.dot_general(a, b, dims, preferred_element_type=F32)


def halves(value):
    high = value.astype(BF16)
    return high, (value - high.astype(F32)).astype(BF16)


def blocks(chip, core, width):
    owner = [
        lax.rem(chip + step, 4) * 2 + which for which in (core, 1 - core) for step in (0, 3, 1, 2)
    ]
    return lambda slot: pl.ds(pl.multiple_of(owner[slot] * width, 128), width)


def body(
    micro, heads, n_section,
    x_hbm, u_hbm, scores_hbm, wv_hbm, wo_hbm, feedback_hbm, basis_hbm,
    u, x, wv, att, va, vg, gow_first, gvw, new, factors_in, basis,
    wo, wv_far, scores, feedback,
    att_t, ag, vg_far, parts, out_stage, in_hop, in_left, in_right, factors,
    load_sem, send_sem, recv_sem, begun_sem,
):
    rows, width = u_hbm.shape
    length = rows // micro
    quarter = length // 2
    inner = wv_hbm.shape[1]
    head = inner // heads

    s = lax.axis_index("section")
    t = lax.axis_index("tensor")
    chip, core = t // 2, lax.rem(t, 2)

    def place(step, which):
        return lax.rem(chip + step, 4) * 2 + which

    right = (s, place(1, core))
    left = (s, place(3, core))
    sister = (s, place(0, 1 - core))

    row_first, row_last = lax.rem(s, ROW) == 0, lax.rem(s, ROW) == ROW - 1

    def section(step):
        return lax.rem(s + n_section + step, n_section), t

    block_of = blocks(chip, core, width)

    def batch(m):
        return pl.ds(m * length, length)

    def first(m):
        return pl.ds(m * length, quarter)

    def second(m):
        return pl.ds(m * length + quarter, quarter)

    loads = []

    def load(src, dst):
        copy = pltpu.make_async_copy(src, dst, load_sem.at[len(loads)])
        copy.start()
        loads.append(copy)
        return copy

    got_scores = load(scores_hbm, scores)
    got_u = load(u_hbm, u.at[0])
    got_wo = load(wo_hbm, wo)
    got_wv = load(wv_hbm, wv)
    got_x = load(x_hbm, x.at[0])
    got_feedback = load(feedback_hbm, feedback)
    got_basis = load(basis_hbm, basis)

    barrier = pltpu.get_barrier_semaphore()
    for peer in (right, left, sister):
        pl.semaphore_signal(barrier, inc=1, device_id=peer, device_id_type=MESH)

    @pl.when(row_first)
    def _():
        pl.semaphore_signal(barrier, inc=1, device_id=section(ROW - 1), device_id_type=MESH)

    pl.semaphore_signal(
        barrier, inc=1, device_id=(jnp.where(row_last, section(ROW)[0], section(1)[0]), t),
        device_id_type=MESH,
    )
    pl.semaphore_wait(barrier, 4 + row_last.astype(jnp.int32) * 2 - row_first.astype(jnp.int32))

    @pl.when(row_last)
    def _():
        pl.semaphore_signal(begun_sem, inc=1, device_id=section(1 - ROW), device_id_type=MESH)

    sent = []

    def send(src, dst, device):
        i = len(sent)
        copy = pltpu.make_async_remote_copy(
            src_ref=src, dst_ref=dst, send_sem=send_sem.at[i], recv_sem=recv_sem.at[i],
            device_id=device, device_id_type=MESH,
        )
        copy.start()
        sent.append(copy)
        return copy

    def arrive(*copies):
        for copy in copies:
            copy.wait_recv()

    def spread(src, dst, m):
        return (
            send(src.at[first(m)], dst.at[1, first(m)], right),
            send(src.at[second(m)], dst.at[2, second(m)], left),
            send(src.at[second(m)], dst.at[1, second(m)], right),
            send(src.at[first(m)], dst.at[2, first(m)], left),
        )

    def relay(dst, m, copies):
        arrive(copies[0])
        onward = send(dst.at[1, first(m)], dst.at[3, first(m)], right)
        arrive(copies[1])
        return onward, send(dst.at[2, second(m)], dst.at[3, second(m)], left)

    def share(dst, slot, rows_):
        return send(dst.at[slot, rows_], dst.at[slot + 4, rows_], sister)

    u_out = [spread(u_hbm, u, 0)]
    u_own = send(u_hbm, u.at[4], sister)
    far = []
    for step in range(4):
        block = pl.ds(pl.multiple_of(place(step, 1 - core) * width, 128), width)
        far.append(send(wv_hbm.at[block], wv_far.at[step], sister))

    got_scores.wait()
    query = lax.broadcasted_iota(jnp.int32, (length, length), 0)
    key = lax.broadcasted_iota(jnp.int32, (length, length), 1)
    causal = key <= query
    for i in range(micro * heads):
        raised = jnp.where(causal, scores[i].astype(F32), -1e30)
        largest = jnp.max(raised, axis=-1, keepdims=True)
        powers = jnp.where(causal, jnp.exp(raised - largest), 0.0)
        probs = powers / jnp.sum(powers, axis=-1, keepdims=True)
        att[i] = probs.astype(BF16)
        att_t[i] = probs.T.astype(BF16)

    def add_u(m, *slots):
        total = ag[batch(m)]
        for slot in slots:
            total = total + dot(u[slot, batch(m)], wo[:, block_of(slot)], NT)
        ag[batch(m)] = total

    got_u.wait()
    got_wo.wait()
    ag[...] = dot(u[0], wo[:, block_of(0)], NT)

    def value_grad(m):
        for h in range(heads):
            columns = pl.ds(h * head, head)
            grad = dot(att_t[m * heads + h], ag[batch(m), columns].astype(BF16))
            vg[batch(m), columns] = grad.astype(BF16)
        return send(vg.at[batch(m)], vg_far.at[batch(m)], sister)

    def partial(m, step):
        block = pl.ds(pl.multiple_of(place(step, core) * width, 128), width)
        near = dot(vg[batch(m)], wv[block, :], NT)
        return near + dot(vg_far[batch(m)], wv_far[step], NT)

    def begin_sums(m):
        out_stage[0, batch(m)] = partial(m, 2).astype(BF16)
        hops = (
            send(out_stage.at[0, first(m)], in_hop.at[first(m)], right),
            send(out_stage.at[0, second(m)], in_hop.at[second(m)], left),
        )
        parts[1, batch(m)] = partial(m, 1)
        out_stage[1, second(m)] = parts[1, second(m)].astype(BF16)
        ends = [send(out_stage.at[1, second(m)], in_left.at[second(m)], right)]
        parts[2, batch(m)] = partial(m, 3)
        out_stage[2, first(m)] = parts[2, first(m)].astype(BF16)
        ends.append(send(out_stage.at[2, first(m)], in_right.at[first(m)], left))
        parts[0, batch(m)] = partial(m, 0)
        return hops, ends

    def end_sums(m, hops, ends):
        arrive(hops[0])
        out_stage[1, first(m)] = (parts[1, first(m)] + in_hop[first(m)].astype(F32)).astype(BF16)
        ends.append(send(out_stage.at[1, first(m)], in_left.at[first(m)], right))
        arrive(hops[1])
        out_stage[2, second(m)] = (parts[2, second(m)] + in_hop[second(m)].astype(F32)).astype(BF16)
        ends.append(send(out_stage.at[2, second(m)], in_right.at[second(m)], left))

    def gather_u(m, copies, onward):
        arrive(*copies[2:])
        shared = share(u, 1, batch(m)), share(u, 2, batch(m))
        add_u(m, 1, 2)
        arrive(*shared)
        add_u(m, 5, 6)
        arrive(*onward)
        shared = share(u, 3, batch(m))
        add_u(m, 3)
        arrive(shared)
        add_u(m, 7)
        return value_grad(m)

    u_on = [relay(u, 0, u_out[0])]
    u_out.append(spread(u_hbm, u, 1))
    arrive(u_own)
    ag[...] += dot(u[4], wo[:, block_of(4)], NT)
    vg_copy = gather_u(0, u_out[0], u_on[0])
    u_on.append(relay(u, 1, u_out[1]))
    got_wv.wait()
    arrive(vg_copy, *far)
    hops0, ends0 = begin_sums(0)
    x_out = [spread(x_hbm, x, 0)]
    x_own = send(x_hbm, x.at[4], sister)
    vg_copy = gather_u(1, u_out[1], u_on[1])
    end_sums(0, hops0, ends0)
    arrive(vg_copy)
    hops1, ends1 = begin_sums(1)

    def add_x(m, *slots):
        total = va[batch(m)]
        for slot in slots:
            total = total + dot(x[slot, batch(m)], wv[block_of(slot), :])
        va[batch(m)] = total

    def grad_value(slot):
        gvw[slot] = dot(x[slot], vg[...], TN).astype(BF16)

    x_on = [relay(x, 0, x_out[0])]
    got_x.wait()
    va[...] = dot(x[0], wv[block_of(0), :])
    grad_value(0)
    arrive(x_own)
    va[...] += dot(x[4], wv[block_of(4), :])
    grad_value(4)
    arrive(*x_out[0][2:])
    shared = share(x, 1, batch(0)), share(x, 2, batch(0))
    add_x(0, 1, 2)
    arrive(*shared)
    add_x(0, 5, 6)
    got_feedback.wait()
    got_basis.wait()
    basis_high, basis_low = halves(basis[...])

    def compress(m, ends):
        arrive(*ends)
        carried = feedback[batch(m)] + u[0, batch(m)].astype(F32) + parts[0, batch(m)]
        carried = carried + in_left[batch(m)].astype(F32) + in_right[batch(m)].astype(F32)
        high, low = halves(carried)
        found = dot(high, basis_high) + dot(low, basis_high) + dot(high, basis_low)
        own = found.astype(BF16)
        factors[batch(m)] = own
        new[batch(m)] = carried - (dot(own, basis_high, NT) + dot(own, basis_low, NT))

    compress(0, ends0)
    end_sums(1, hops1, ends1)
    x_out.append(spread(x_hbm, x, 1))
    compress(1, ends1)

    arrive(*x_on[0])
    shared = share(x, 3, batch(0))
    add_x(0, 3)
    arrive(shared)
    add_x(0, 7)
    x_on.append(relay(x, 1, x_out[1]))

    @pl.when(row_first)
    def _():
        pl.semaphore_wait(begun_sem, 1)

    factor_copy = send(factors, factors_in, section(-1))
    mixed = attended(0, heads, va, att)
    for slot in range(8):
        gow_first[slot] = dot(mixed, u[slot, batch(0)])

    arrive(*x_out[1][2:])
    shared = share(x, 1, batch(1)), share(x, 2, batch(1))
    add_x(1, 1, 2)
    grad_value(1)
    grad_value(2)
    arrive(*shared)
    add_x(1, 5, 6)
    grad_value(5)
    grad_value(6)

    arrive(x_on[1][0])
    last = [share(x, 3, first(1))]
    arrive(x_on[1][1])
    last.append(share(x, 3, second(1)))
    add_x(1, 3)
    grad_value(3)
    arrive(factor_copy, *last)
    for copy in sent:
        copy.wait_send()


def attended(m, heads, va, att):
    length = att.shape[1]
    head = va.shape[1] // heads
    found = []
    for h in range(heads):
        value = va[pl.ds(m * length, length), pl.ds(h * head, head)]
        found.append(dot(value.T.astype(BF16), att[m * heads + h], NT).astype(BF16))
    return jnp.concatenate(found, axis=0)


def finish(
    micro, heads, n_section, u, x, wv, att, va, vg, gow_first, gvw, new, factors_in, basis,
    gow_hbm, gvw_hbm, new_hbm, rebuilt_hbm, last, gow, total, rebuilt, store_sem,
):
    width = u.shape[2]
    length = att.shape[1]
    s = lax.axis_index("section")
    t = lax.axis_index("tensor")
    block_of = blocks(t // 2, lax.rem(t, 2), width)
    stores = []

    def store(src, dst):
        copy = pltpu.make_async_copy(src, dst, store_sem.at[len(stores)])
        copy.start()
        stores.append(copy)

    for slot in range(7):
        store(gvw.at[slot], gvw_hbm.at[block_of(slot)])
    store(new, new_hbm)

    rows = pl.ds((micro - 1) * length, length)
    total[rows] = va[rows] + dot(x[7, rows], wv[block_of(7), :])
    mixed = attended(micro - 1, heads, total, att)
    for slot in range(8):
        gow[slot] = (gow_first[slot] + dot(mixed, u[slot, rows])).astype(BF16)
        store(gow.at[slot], gow_hbm.at[:, block_of(slot)])
    basis_high, basis_low = halves(basis[...])
    arrived = factors_in[...]
    built = dot(arrived, basis_high, NT) + dot(arrived, basis_low, NT)
    rebuilt[...] = jnp.where(s == n_section - 1, 0.0, built).astype(BF16)
    store(rebuilt, rebuilt_hbm)
    last[...] = dot(x[7], vg[...], TN).astype(BF16)
    store(last, gvw_hbm.at[block_of(7)])
    for copy in stores:
        copy.wait()


def on_device(n_section, layer_input, upstream, scores, value_weight, out_weight, feedback, basis):
    _, micro, length, width = layer_input.shape
    rows = micro * length
    heads = scores.shape[2]
    model, inner = value_weight.shape[1:]
    rank = basis.shape[1]
    vmem = pltpu.VMEM
    anywhere = pl.BlockSpec(memory_space=pl.ANY)
    whole = pl.BlockSpec(memory_space=vmem)
    held = pl.pallas_call(
        functools.partial(body, micro, heads, n_section),
        out_shape=(
            vmem((8, rows, width), BF16),
            vmem((8, rows, width), BF16),
            vmem((model, inner), BF16),
            vmem((micro * heads, length, length), BF16),
            vmem((rows, inner), F32),
            vmem((rows, inner), BF16),
            vmem((8, inner, width), F32),
            vmem((8, width, inner), BF16),
            vmem((rows, width), F32),
            vmem((rows, rank), BF16),
            vmem((width, rank), F32),
        ),
        in_specs=[anywhere] * 7,
        out_specs=(whole,) * 11,
        scratch_shapes=[
            vmem((inner, model), BF16),
            vmem((4, width, inner), BF16),
            vmem((micro * heads, length, length), BF16),
            vmem((rows, width), F32),
            vmem((micro * heads, length, length), BF16),
            vmem((rows, inner), F32),
            vmem((rows, inner), BF16),
            vmem((3, rows, width), F32),
            vmem((3, rows, width), BF16),
            vmem((rows, width), BF16),
            vmem((rows, width), BF16),
            vmem((rows, width), BF16),
            vmem((rows, rank), BF16),
            pltpu.SemaphoreType.DMA((7,)),
            pltpu.SemaphoreType.DMA((80,)),
            pltpu.SemaphoreType.DMA((80,)),
            pltpu.SemaphoreType.REGULAR,
        ],
        compiler_params=pltpu.CompilerParams(
            collective_id=0, has_side_effects=True, vmem_limit_bytes=40 << 20
        ),
    )(*(
        pltpu.with_memory_space_constraint(value, pltpu.HBM)
        for value in (
            layer_input.reshape(rows, width),
            upstream.reshape(rows, width),
            scores.reshape(micro * heads, length, length),
            value_weight[0],
            out_weight[0],
            feedback.reshape(rows, width),
            basis,
        )
    ))
    gow, gvw, new, rebuilt = pl.pallas_call(
        functools.partial(finish, micro, heads, n_section),
        out_shape=(
            jax.ShapeDtypeStruct((inner, model), BF16),
            jax.ShapeDtypeStruct((model, inner), BF16),
            jax.ShapeDtypeStruct((rows, width), F32),
            jax.ShapeDtypeStruct((rows, width), BF16),
        ),
        in_specs=[whole] * 11,
        out_specs=(anywhere,) * 4,
        scratch_shapes=[
            vmem((width, inner), BF16),
            vmem((8, inner, width), BF16),
            vmem((rows, inner), F32),
            vmem((rows, width), BF16),
            pltpu.SemaphoreType.DMA((18,)),
        ],
        compiler_params=pltpu.CompilerParams(vmem_limit_bytes=16 << 20),
    )(*(pltpu.with_memory_space_constraint(value, pltpu.VMEM) for value in held))
    shape = (1, micro, length, width)
    return gow[None], gvw[None], new.reshape(shape), rebuilt.reshape(shape)


def solution(mesh):
    in_specs = (
        P("section", None, None, "tensor"),
        P("section", None, None, "tensor"),
        P("section", None, "tensor", None, None),
        P("section", None, "tensor"),
        P("section", "tensor", None),
        P("section", None, None, "tensor"),
        P("tensor", None),
    )
    out_specs = (
        P("section", "tensor", None),
        P("section", None, "tensor"),
        P("section", None, None, "tensor"),
        P("section", None, None, "tensor"),
    )
    return jax.shard_map(
        functools.partial(on_device, mesh.shape["section"]),
        mesh=mesh, in_specs=in_specs, out_specs=out_specs, check_vma=False,
    )
```

```python
import functools

import jax
import jax.numpy as jnp
from jax import lax
from jax.experimental import pallas as pl
from jax.experimental.pallas import tpu as pltpu
from jax.sharding import PartitionSpec as P

MESH = pl.DeviceIdType.MESH
NT = (((1,), (1,)), ((), ()))
TN = (((0,), (0,)), ((), ()))
ROW = 8
F32 = jnp.float32
BF16 = jnp.bfloat16


def dot(a, b, dims=(((1,), (0,)), ((), ()))):
    return lax.dot_general(a, b, dims, preferred_element_type=F32)


def halves(value):
    high = value.astype(BF16)
    return high, (value - high.astype(F32)).astype(BF16)


def blocks(chip, core, width):
    owner = [
        lax.rem(chip + step, 4) * 2 + which for which in (core, 1 - core) for step in (0, 3, 1, 2)
    ]
    return lambda slot: pl.ds(pl.multiple_of(owner[slot] * width, 128), width)


def body(
    micro, heads, n_section,
    x_hbm, u_hbm, scores_hbm, wv_hbm, wo_hbm, feedback_hbm, basis_hbm,
    u, x, wv, att, va, vg, gow_first, gvw, new, factors_in, basis,
    wo, wv_far, scores, feedback,
    att_t, ag, vg_far, parts, out_stage, in_hop, in_left, in_right, factors,
    load_sem, send_sem, recv_sem, begun_sem,
):
    rows, width = u_hbm.shape
    length = rows // micro
    quarter = length // 2
    inner = wv_hbm.shape[1]
    head = inner // heads

    s = lax.axis_index("section")
    t = lax.axis_index("tensor")
    chip, core = t // 2, lax.rem(t, 2)

    def place(step, which):
        return lax.rem(chip + step, 4) * 2 + which

    right = (s, place(1, core))
    left = (s, place(3, core))
    sister = (s, place(0, 1 - core))

    row_first, row_last = lax.rem(s, ROW) == 0, lax.rem(s, ROW) == ROW - 1

    def section(step):
        return lax.rem(s + n_section + step, n_section), t

    block_of = blocks(chip, core, width)

    def batch(m):
        return pl.ds(m * length, length)

    def first(m):
        return pl.ds(m * length, quarter)

    def second(m):
        return pl.ds(m * length + quarter, quarter)

    loads = []

    def load(src, dst):
        copy = pltpu.make_async_copy(src, dst, load_sem.at[len(loads)])
        copy.start()
        loads.append(copy)
        return copy

    got_scores = load(scores_hbm, scores)
    got_u = load(u_hbm, u.at[0])
    got_wo = load(wo_hbm, wo)
    got_wv = load(wv_hbm, wv)
    got_x = load(x_hbm, x.at[0])
    got_feedback = load(feedback_hbm, feedback)
    got_basis = load(basis_hbm, basis)

    barrier = pltpu.get_barrier_semaphore()
    for peer in (right, left, sister):
        pl.semaphore_signal(barrier, inc=1, device_id=peer, device_id_type=MESH)

    @pl.when(row_first)
    def _():
        pl.semaphore_signal(barrier, inc=1, device_id=section(ROW - 1), device_id_type=MESH)

    pl.semaphore_signal(
        barrier, inc=1, device_id=(jnp.where(row_last, section(ROW)[0], section(1)[0]), t),
        device_id_type=MESH,
    )
    pl.semaphore_wait(barrier, 4 + row_last.astype(jnp.int32) * 2 - row_first.astype(jnp.int32))

    @pl.when(row_last)
    def _():
        pl.semaphore_signal(begun_sem, inc=1, device_id=section(1 - ROW), device_id_type=MESH)

    sent = []

    def send(src, dst, device):
        i = len(sent)
        copy = pltpu.make_async_remote_copy(
            src_ref=src, dst_ref=dst, send_sem=send_sem.at[i], recv_sem=recv_sem.at[i],
            device_id=device, device_id_type=MESH,
        )
        copy.start()
        sent.append(copy)
        return copy

    def arrive(*copies):
        for copy in copies:
            copy.wait_recv()

    def spread_first(src, dst, m):
        return (
            send(src.at[first(m)], dst.at[1, first(m)], right),
            send(src.at[second(m)], dst.at[2, second(m)], left),
        )

    def spread_second(src, dst, m):
        return (
            send(src.at[second(m)], dst.at[1, second(m)], right),
            send(src.at[first(m)], dst.at[2, first(m)], left),
        )

    def spread(src, dst, m):
        return spread_first(src, dst, m) + spread_second(src, dst, m)

    def relay(dst, m, copies):
        arrive(copies[0])
        onward = send(dst.at[1, first(m)], dst.at[3, first(m)], right)
        arrive(copies[1])
        return onward, send(dst.at[2, second(m)], dst.at[3, second(m)], left)

    def share(dst, slot, rows_):
        return send(dst.at[slot, rows_], dst.at[slot + 4, rows_], sister)

    u_out = [spread(u_hbm, u, 0)]
    u_own = send(u_hbm, u.at[4], sister)
    far = []
    for step in range(4):
        block = pl.ds(pl.multiple_of(place(step, 1 - core) * width, 128), width)
        far.append(send(wv_hbm.at[block], wv_far.at[step], sister))

    u_out.append(spread_first(u_hbm, u, 1))
    got_scores.wait()
    query = lax.broadcasted_iota(jnp.int32, (length, length), 0)
    key = lax.broadcasted_iota(jnp.int32, (length, length), 1)
    causal = key <= query
    for i in range(micro * heads):
        raised = jnp.where(causal, scores[i].astype(F32), -1e30)
        largest = jnp.max(raised, axis=-1, keepdims=True)
        powers = jnp.where(causal, jnp.exp(raised - largest), 0.0)
        probs = powers / jnp.sum(powers, axis=-1, keepdims=True)
        att[i] = probs.astype(BF16)
        att_t[i] = probs.T.astype(BF16)

    def add_u(m, *slots):
        total = ag[batch(m)]
        for slot in slots:
            total = total + dot(u[slot, batch(m)], wo[:, block_of(slot)], NT)
        ag[batch(m)] = total

    got_u.wait()
    got_wo.wait()
    ag[...] = dot(u[0], wo[:, block_of(0)], NT)

    def value_grad(m):
        for h in range(heads):
            columns = pl.ds(h * head, head)
            grad = dot(att_t[m * heads + h], ag[batch(m), columns].astype(BF16))
            vg[batch(m), columns] = grad.astype(BF16)
        return send(vg.at[batch(m)], vg_far.at[batch(m)], sister)

    def partial(m, step):
        block = pl.ds(pl.multiple_of(place(step, core) * width, 128), width)
        near = dot(vg[batch(m)], wv[block, :], NT)
        return near + dot(vg_far[batch(m)], wv_far[step], NT)

    def begin_sums(m):
        out_stage[0, batch(m)] = partial(m, 2).astype(BF16)
        hops = (
            send(out_stage.at[0, first(m)], in_hop.at[first(m)], right),
            send(out_stage.at[0, second(m)], in_hop.at[second(m)], left),
        )
        parts[1, batch(m)] = partial(m, 1)
        out_stage[1, second(m)] = parts[1, second(m)].astype(BF16)
        ends = [send(out_stage.at[1, second(m)], in_left.at[second(m)], right)]
        parts[2, batch(m)] = partial(m, 3)
        out_stage[2, first(m)] = parts[2, first(m)].astype(BF16)
        ends.append(send(out_stage.at[2, first(m)], in_right.at[first(m)], left))
        parts[0, batch(m)] = partial(m, 0)
        return hops, ends

    def end_sums(m, hops, ends):
        arrive(hops[0])
        out_stage[1, first(m)] = (parts[1, first(m)] + in_hop[first(m)].astype(F32)).astype(BF16)
        ends.append(send(out_stage.at[1, first(m)], in_left.at[first(m)], right))
        arrive(hops[1])
        out_stage[2, second(m)] = (parts[2, second(m)] + in_hop[second(m)].astype(F32)).astype(BF16)
        ends.append(send(out_stage.at[2, second(m)], in_right.at[second(m)], left))

    def gather_u(m, copies, onward):
        arrive(*copies[2:])
        shared = share(u, 1, batch(m)), share(u, 2, batch(m))
        add_u(m, 1, 2)
        arrive(*shared)
        add_u(m, 5, 6)
        arrive(*onward)
        shared = share(u, 3, batch(m))
        add_u(m, 3)
        arrive(shared)
        add_u(m, 7)
        return value_grad(m)

    u_on = [relay(u, 0, u_out[0])]
    u_out[1] += spread_second(u_hbm, u, 1)
    arrive(u_own)
    ag[...] += dot(u[4], wo[:, block_of(4)], NT)
    u_on.append(relay(u, 1, u_out[1]))
    x_out = [spread(x_hbm, x, 0)]
    x_own = send(x_hbm, x.at[4], sister)
    vg_copy = gather_u(0, u_out[0], u_on[0])
    got_wv.wait()
    arrive(vg_copy, *far)
    hops0, ends0 = begin_sums(0)
    vg_copy = gather_u(1, u_out[1], u_on[1])
    arrive(vg_copy)
    hops1, ends1 = begin_sums(1)
    end_sums(0, hops0, ends0)
    def add_x(m, *slots):
        total = va[batch(m)]
        for slot in slots:
            total = total + dot(x[slot, batch(m)], wv[block_of(slot), :])
        va[batch(m)] = total

    def grad_value(slot):
        gvw[slot] = dot(x[slot], vg[...], TN).astype(BF16)

    end_sums(1, hops1, ends1)
    x_on = [relay(x, 0, x_out[0])]
    x_out.append(spread(x_hbm, x, 1))
    got_x.wait()
    va[...] = dot(x[0], wv[block_of(0), :])
    grad_value(0)
    arrive(x_own)
    va[...] += dot(x[4], wv[block_of(4), :])
    grad_value(4)
    arrive(*x_out[0][2:])
    shared0 = share(x, 1, batch(0)), share(x, 2, batch(0))
    add_x(0, 1, 2)
    arrive(*shared0)
    add_x(0, 5, 6)
    got_feedback.wait()
    got_basis.wait()
    basis_high, basis_low = halves(basis[...])

    def compress(m, ends):
        arrive(*ends)
        carried = feedback[batch(m)] + u[0, batch(m)].astype(F32) + parts[0, batch(m)]
        carried = carried + in_left[batch(m)].astype(F32) + in_right[batch(m)].astype(F32)
        high, low = halves(carried)
        found = dot(high, basis_high) + dot(low, basis_high) + dot(high, basis_low)
        own = found.astype(BF16)
        factors[batch(m)] = own
        new[batch(m)] = carried - (dot(own, basis_high, NT) + dot(own, basis_low, NT))

    compress(0, ends0)
    compress(1, ends1)
    arrive(*x_on[0])
    shared3 = share(x, 3, batch(0))
    add_x(0, 3)
    arrive(shared3)
    add_x(0, 7)
    x_on.append(relay(x, 1, x_out[1]))

    @pl.when(row_first)
    def _():
        pl.semaphore_wait(begun_sem, 1)

    factor_copy = send(factors, factors_in, section(-1))
    mixed = attended(0, heads, va, att)
    for slot in range(8):
        gow_first[slot] = dot(mixed, u[slot, batch(0)])
    arrive(*x_out[1][2:])
    shared1 = share(x, 1, batch(1)), share(x, 2, batch(1))
    add_x(1, 1, 2)
    grad_value(1)
    grad_value(2)
    arrive(*shared1)
    add_x(1, 5, 6)
    grad_value(5)
    grad_value(6)
    arrive(x_on[1][0])
    last = [share(x, 3, first(1))]
    arrive(x_on[1][1])
    last.append(share(x, 3, second(1)))
    add_x(1, 3)
    grad_value(3)
    arrive(factor_copy, *last)
    for copy in sent:
        copy.wait_send()


def attended(m, heads, va, att):
    length = att.shape[1]
    head = va.shape[1] // heads
    found = []
    for h in range(heads):
        value = va[pl.ds(m * length, length), pl.ds(h * head, head)]
        found.append(dot(value.T.astype(BF16), att[m * heads + h], NT).astype(BF16))
    return jnp.concatenate(found, axis=0)


def finish(
    micro, heads, n_section, u, x, wv, att, va, vg, gow_first, gvw, new, factors_in, basis,
    gow_hbm, gvw_hbm, new_hbm, rebuilt_hbm, last, gow, total, rebuilt, store_sem,
):
    width = u.shape[2]
    length = att.shape[1]
    s = lax.axis_index("section")
    t = lax.axis_index("tensor")
    block_of = blocks(t // 2, lax.rem(t, 2), width)
    stores = []

    def store(src, dst):
        copy = pltpu.make_async_copy(src, dst, store_sem.at[len(stores)])
        copy.start()
        stores.append(copy)

    for slot in range(7):
        store(gvw.at[slot], gvw_hbm.at[block_of(slot)])
    store(new, new_hbm)

    rows = pl.ds((micro - 1) * length, length)
    total[rows] = va[rows] + dot(x[7, rows], wv[block_of(7), :])
    mixed = attended(micro - 1, heads, total, att)
    for slot in range(8):
        gow[slot] = (gow_first[slot] + dot(mixed, u[slot, rows])).astype(BF16)
        store(gow.at[slot], gow_hbm.at[:, block_of(slot)])
    basis_high, basis_low = halves(basis[...])
    arrived = factors_in[...]
    built = dot(arrived, basis_high, NT) + dot(arrived, basis_low, NT)
    rebuilt[...] = jnp.where(s == n_section - 1, 0.0, built).astype(BF16)
    store(rebuilt, rebuilt_hbm)
    last[...] = dot(x[7], vg[...], TN).astype(BF16)
    store(last, gvw_hbm.at[block_of(7)])
    for copy in stores:
        copy.wait()


def on_device(n_section, layer_input, upstream, scores, value_weight, out_weight, feedback, basis):
    _, micro, length, width = layer_input.shape
    rows = micro * length
    heads = scores.shape[2]
    model, inner = value_weight.shape[1:]
    rank = basis.shape[1]
    vmem = pltpu.VMEM
    anywhere = pl.BlockSpec(memory_space=pl.ANY)
    whole = pl.BlockSpec(memory_space=vmem)
    held = pl.pallas_call(
        functools.partial(body, micro, heads, n_section),
        out_shape=(
            vmem((8, rows, width), BF16),
            vmem((8, rows, width), BF16),
            vmem((model, inner), BF16),
            vmem((micro * heads, length, length), BF16),
            vmem((rows, inner), F32),
            vmem((rows, inner), BF16),
            vmem((8, inner, width), F32),
            vmem((8, width, inner), BF16),
            vmem((rows, width), F32),
            vmem((rows, rank), BF16),
            vmem((width, rank), F32),
        ),
        in_specs=[anywhere] * 7,
        out_specs=(whole,) * 11,
        scratch_shapes=[
            vmem((inner, model), BF16),
            vmem((4, width, inner), BF16),
            vmem((micro * heads, length, length), BF16),
            vmem((rows, width), F32),
            vmem((micro * heads, length, length), BF16),
            vmem((rows, inner), F32),
            vmem((rows, inner), BF16),
            vmem((3, rows, width), F32),
            vmem((3, rows, width), BF16),
            vmem((rows, width), BF16),
            vmem((rows, width), BF16),
            vmem((rows, width), BF16),
            vmem((rows, rank), BF16),
            pltpu.SemaphoreType.DMA((7,)),
            pltpu.SemaphoreType.DMA((80,)),
            pltpu.SemaphoreType.DMA((80,)),
            pltpu.SemaphoreType.REGULAR,
        ],
        compiler_params=pltpu.CompilerParams(
            collective_id=0, has_side_effects=True, vmem_limit_bytes=40 << 20
        ),
    )(*(
        pltpu.with_memory_space_constraint(value, pltpu.HBM)
        for value in (
            layer_input.reshape(rows, width),
            upstream.reshape(rows, width),
            scores.reshape(micro * heads, length, length),
            value_weight[0],
            out_weight[0],
            feedback.reshape(rows, width),
            basis,
        )
    ))
    gow, gvw, new, rebuilt = pl.pallas_call(
        functools.partial(finish, micro, heads, n_section),
        out_shape=(
            jax.ShapeDtypeStruct((inner, model), BF16),
            jax.ShapeDtypeStruct((model, inner), BF16),
            jax.ShapeDtypeStruct((rows, width), F32),
            jax.ShapeDtypeStruct((rows, width), BF16),
        ),
        in_specs=[whole] * 11,
        out_specs=(anywhere,) * 4,
        scratch_shapes=[
            vmem((width, inner), BF16),
            vmem((8, inner, width), BF16),
            vmem((rows, inner), F32),
            vmem((rows, width), BF16),
            pltpu.SemaphoreType.DMA((18,)),
        ],
        compiler_params=pltpu.CompilerParams(vmem_limit_bytes=16 << 20),
    )(*(pltpu.with_memory_space_constraint(value, pltpu.VMEM) for value in held))
    shape = (1, micro, length, width)
    return gow[None], gvw[None], new.reshape(shape), rebuilt.reshape(shape)


def solution(mesh):
    in_specs = (
        P("section", None, None, "tensor"),
        P("section", None, None, "tensor"),
        P("section", None, "tensor", None, None),
        P("section", None, "tensor"),
        P("section", "tensor", None),
        P("section", None, None, "tensor"),
        P("tensor", None),
    )
    out_specs = (
        P("section", "tensor", None),
        P("section", None, "tensor"),
        P("section", None, None, "tensor"),
        P("section", None, None, "tensor"),
    )
    return jax.shard_map(
        functools.partial(on_device, mesh.shape["section"]),
        mesh=mesh, in_specs=in_specs, out_specs=out_specs, check_vma=False,
    )
```

```python
import functools

import jax
import jax.numpy as jnp
from jax import lax
from jax.experimental import pallas as pl
from jax.experimental.pallas import tpu as pltpu
from jax.sharding import PartitionSpec as P

MESH = pl.DeviceIdType.MESH
NT = (((1,), (1,)), ((), ()))
TN = (((0,), (0,)), ((), ()))
ROW = 8
F32 = jnp.float32
BF16 = jnp.bfloat16


def dot(a, b, dims=(((1,), (0,)), ((), ()))):
    return lax.dot_general(a, b, dims, preferred_element_type=F32)


def halves(value):
    high = value.astype(BF16)
    return high, (value - high.astype(F32)).astype(BF16)


def blocks(chip, core, width):
    owner = [
        lax.rem(chip + step, 4) * 2 + which for which in (core, 1 - core) for step in (0, 3, 1, 2)
    ]
    return lambda slot: pl.ds(pl.multiple_of(owner[slot] * width, 128), width)


def body(
    micro, heads, n_section,
    x_hbm, u_hbm, scores_hbm, wv_hbm, wo_hbm, feedback_hbm, basis_hbm,
    u, x, wv, att, va, vg, gow_first, gvw, new, factors_in, basis,
    wo, wv_far, scores, feedback,
    att_t, ag, vg_far, parts, out_stage, in_hop, in_left, in_right, factors,
    load_sem, send_sem, recv_sem, begun_sem,
):
    rows, width = u_hbm.shape
    length = rows // micro
    quarter = length // 2
    inner = wv_hbm.shape[1]
    head = inner // heads

    s = lax.axis_index("section")
    t = lax.axis_index("tensor")
    chip, core = t // 2, lax.rem(t, 2)

    def place(step, which):
        return lax.rem(chip + step, 4) * 2 + which

    right = (s, place(1, core))
    left = (s, place(3, core))
    sister = (s, place(0, 1 - core))

    row_first, row_last = lax.rem(s, ROW) == 0, lax.rem(s, ROW) == ROW - 1

    def section(step):
        return lax.rem(s + n_section + step, n_section), t

    block_of = blocks(chip, core, width)

    def batch(m):
        return pl.ds(m * length, length)

    def first(m):
        return pl.ds(m * length, quarter)

    def second(m):
        return pl.ds(m * length + quarter, quarter)

    loads = []

    def load(src, dst):
        copy = pltpu.make_async_copy(src, dst, load_sem.at[len(loads)])
        copy.start()
        loads.append(copy)
        return copy

    got_scores = load(scores_hbm, scores)
    got_u = load(u_hbm, u.at[0])
    got_wo = load(wo_hbm, wo)
    got_wv = load(wv_hbm, wv)
    got_x = load(x_hbm, x.at[0])
    got_feedback = load(feedback_hbm, feedback)
    got_basis = load(basis_hbm, basis)

    barrier = pltpu.get_barrier_semaphore()
    for peer in (right, left, sister):
        pl.semaphore_signal(barrier, inc=1, device_id=peer, device_id_type=MESH)

    @pl.when(row_first)
    def _():
        pl.semaphore_signal(barrier, inc=1, device_id=section(ROW - 1), device_id_type=MESH)

    pl.semaphore_signal(
        barrier, inc=1, device_id=(jnp.where(row_last, section(ROW)[0], section(1)[0]), t),
        device_id_type=MESH,
    )
    pl.semaphore_wait(barrier, 4 + row_last.astype(jnp.int32) * 2 - row_first.astype(jnp.int32))

    @pl.when(row_last)
    def _():
        pl.semaphore_signal(begun_sem, inc=1, device_id=section(1 - ROW), device_id_type=MESH)

    sent = []

    def send(src, dst, device):
        i = len(sent)
        copy = pltpu.make_async_remote_copy(
            src_ref=src, dst_ref=dst, send_sem=send_sem.at[i], recv_sem=recv_sem.at[i],
            device_id=device, device_id_type=MESH,
        )
        copy.start()
        sent.append(copy)
        return copy

    def arrive(*copies):
        for copy in copies:
            copy.wait_recv()

    def spread_first(src, dst, m):
        return (
            send(src.at[first(m)], dst.at[1, first(m)], right),
            send(src.at[second(m)], dst.at[2, second(m)], left),
        )

    def spread_second(src, dst, m):
        return (
            send(src.at[second(m)], dst.at[1, second(m)], right),
            send(src.at[first(m)], dst.at[2, first(m)], left),
        )

    def spread(src, dst, m):
        return spread_first(src, dst, m) + spread_second(src, dst, m)

    def relay(dst, m, copies):
        arrive(copies[0])
        onward = send(dst.at[1, first(m)], dst.at[3, first(m)], right)
        arrive(copies[1])
        return onward, send(dst.at[2, second(m)], dst.at[3, second(m)], left)

    def share(dst, slot, rows_):
        return send(dst.at[slot, rows_], dst.at[slot + 4, rows_], sister)

    u_out = [spread(u_hbm, u, 0)]
    u_own = send(u_hbm, u.at[4], sister)
    far = []
    for step in range(4):
        block = pl.ds(pl.multiple_of(place(step, 1 - core) * width, 128), width)
        far.append(send(wv_hbm.at[block], wv_far.at[step], sister))

    u_out.append(spread_first(u_hbm, u, 1))
    got_scores.wait()
    query = lax.broadcasted_iota(jnp.int32, (length, length), 0)
    key = lax.broadcasted_iota(jnp.int32, (length, length), 1)
    causal = key <= query
    for i in range(micro * heads):
        raised = jnp.where(causal, scores[i].astype(F32), -1e30)
        largest = jnp.max(raised, axis=-1, keepdims=True)
        powers = jnp.where(causal, jnp.exp(raised - largest), 0.0)
        probs = powers / jnp.sum(powers, axis=-1, keepdims=True)
        att[i] = probs.astype(BF16)
        att_t[i] = probs.T.astype(BF16)

    def add_u(m, *slots):
        total = ag[batch(m)]
        for slot in slots:
            total = total + dot(u[slot, batch(m)], wo[:, block_of(slot)], NT)
        ag[batch(m)] = total

    got_u.wait()
    got_wo.wait()
    ag[...] = dot(u[0], wo[:, block_of(0)], NT)

    def value_grad(m):
        for h in range(heads):
            columns = pl.ds(h * head, head)
            grad = dot(att_t[m * heads + h], ag[batch(m), columns].astype(BF16))
            vg[batch(m), columns] = grad.astype(BF16)
        return send(vg.at[batch(m)], vg_far.at[batch(m)], sister)

    def partial(m, step):
        block = pl.ds(pl.multiple_of(place(step, core) * width, 128), width)
        near = dot(vg[batch(m)], wv[block, :], NT)
        return near + dot(vg_far[batch(m)], wv_far[step], NT)

    def begin_sums(m):
        out_stage[0, batch(m)] = partial(m, 2).astype(BF16)
        hops = (
            send(out_stage.at[0, first(m)], in_hop.at[first(m)], right),
            send(out_stage.at[0, second(m)], in_hop.at[second(m)], left),
        )
        parts[1, batch(m)] = partial(m, 1)
        out_stage[1, second(m)] = parts[1, second(m)].astype(BF16)
        ends = [send(out_stage.at[1, second(m)], in_left.at[second(m)], right)]
        parts[2, batch(m)] = partial(m, 3)
        out_stage[2, first(m)] = parts[2, first(m)].astype(BF16)
        ends.append(send(out_stage.at[2, first(m)], in_right.at[first(m)], left))
        parts[0, batch(m)] = partial(m, 0)
        return hops, ends

    def end_sums(m, hops, ends):
        arrive(hops[0])
        out_stage[1, first(m)] = (parts[1, first(m)] + in_hop[first(m)].astype(F32)).astype(BF16)
        ends.append(send(out_stage.at[1, first(m)], in_left.at[first(m)], right))
        arrive(hops[1])
        out_stage[2, second(m)] = (parts[2, second(m)] + in_hop[second(m)].astype(F32)).astype(BF16)
        ends.append(send(out_stage.at[2, second(m)], in_right.at[second(m)], left))

    def gather_u(m, copies, onward):
        arrive(*copies[2:])
        shared = share(u, 1, batch(m)), share(u, 2, batch(m))
        add_u(m, 1, 2)
        arrive(*shared)
        add_u(m, 5, 6)
        arrive(*onward)
        shared = share(u, 3, batch(m))
        add_u(m, 3)
        arrive(shared)
        add_u(m, 7)
        return value_grad(m)

    u_on = [relay(u, 0, u_out[0])]
    u_out[1] += spread_second(u_hbm, u, 1)
    arrive(u_own)
    ag[...] += dot(u[4], wo[:, block_of(4)], NT)
    u_on.append(relay(u, 1, u_out[1]))
    x_out = [spread(x_hbm, x, 0)]
    x_own = send(x_hbm, x.at[4], sister)
    vg_copy = gather_u(0, u_out[0], u_on[0])
    got_wv.wait()
    arrive(vg_copy, *far)
    hops0, ends0 = begin_sums(0)
    vg_copy = gather_u(1, u_out[1], u_on[1])
    arrive(vg_copy)
    hops1, ends1 = begin_sums(1)
    end_sums(0, hops0, ends0)
    def add_x(m, *slots):
        total = va[batch(m)]
        for slot in slots:
            total = total + dot(x[slot, batch(m)], wv[block_of(slot), :])
        va[batch(m)] = total

    def grad_value(slot):
        gvw[slot] = dot(x[slot], vg[...], TN).astype(BF16)

    end_sums(1, hops1, ends1)
    x_on = [relay(x, 0, x_out[0])]
    x_out.append(spread(x_hbm, x, 1))
    got_x.wait()
    va[...] = dot(x[0], wv[block_of(0), :])
    grad_value(0)
    arrive(x_own)
    va[...] += dot(x[4], wv[block_of(4), :])
    grad_value(4)
    arrive(*x_out[0][2:])
    shared0 = share(x, 1, batch(0)), share(x, 2, batch(0))
    add_x(0, 1, 2)
    arrive(*shared0)
    add_x(0, 5, 6)
    got_feedback.wait()
    got_basis.wait()
    basis_high, basis_low = halves(basis[...])

    def compress(m, ends):
        arrive(*ends)
        carried = feedback[batch(m)] + u[0, batch(m)].astype(F32) + parts[0, batch(m)]
        carried = carried + in_left[batch(m)].astype(F32) + in_right[batch(m)].astype(F32)
        high, low = halves(carried)
        found = dot(high, basis_high) + dot(low, basis_high) + dot(high, basis_low)
        own = found.astype(BF16)
        factors[batch(m)] = own
        new[batch(m)] = carried - (dot(own, basis_high, NT) + dot(own, basis_low, NT))

    compress(0, ends0)
    compress(1, ends1)
    x_on.append(relay(x, 1, x_out[1]))

    @pl.when(row_first)
    def _():
        pl.semaphore_wait(begun_sem, 1)

    factor_copy = send(factors, factors_in, section(-1))
    arrive(*x_on[0])
    shared3 = share(x, 3, batch(0))
    add_x(0, 3)
    arrive(shared3)
    add_x(0, 7)
    mixed = attended(0, heads, va, att)
    for slot in range(8):
        gow_first[slot] = dot(mixed, u[slot, batch(0)])
    arrive(*x_out[1][2:])
    shared1 = share(x, 1, batch(1)), share(x, 2, batch(1))
    add_x(1, 1, 2)
    grad_value(1)
    grad_value(2)
    arrive(*shared1)
    add_x(1, 5, 6)
    grad_value(5)
    grad_value(6)
    arrive(x_on[1][0])
    last = [share(x, 3, first(1))]
    arrive(x_on[1][1])
    last.append(share(x, 3, second(1)))
    add_x(1, 3)
    grad_value(3)
    arrive(factor_copy, *last)
    for copy in sent:
        copy.wait_send()


def attended(m, heads, va, att):
    length = att.shape[1]
    head = va.shape[1] // heads
    found = []
    for h in range(heads):
        value = va[pl.ds(m * length, length), pl.ds(h * head, head)]
        found.append(dot(value.T.astype(BF16), att[m * heads + h], NT).astype(BF16))
    return jnp.concatenate(found, axis=0)


def finish(
    micro, heads, n_section, u, x, wv, att, va, vg, gow_first, gvw, new, factors_in, basis,
    gow_hbm, gvw_hbm, new_hbm, rebuilt_hbm, last, gow, total, rebuilt, store_sem,
):
    width = u.shape[2]
    length = att.shape[1]
    s = lax.axis_index("section")
    t = lax.axis_index("tensor")
    block_of = blocks(t // 2, lax.rem(t, 2), width)
    stores = []

    def store(src, dst):
        copy = pltpu.make_async_copy(src, dst, store_sem.at[len(stores)])
        copy.start()
        stores.append(copy)

    for slot in range(7):
        store(gvw.at[slot], gvw_hbm.at[block_of(slot)])
    store(new, new_hbm)

    rows = pl.ds((micro - 1) * length, length)
    total[rows] = va[rows] + dot(x[7, rows], wv[block_of(7), :])
    mixed = attended(micro - 1, heads, total, att)
    for slot in range(8):
        gow[slot] = (gow_first[slot] + dot(mixed, u[slot, rows])).astype(BF16)
        store(gow.at[slot], gow_hbm.at[:, block_of(slot)])
    basis_high, basis_low = halves(basis[...])
    arrived = factors_in[...]
    built = dot(arrived, basis_high, NT) + dot(arrived, basis_low, NT)
    rebuilt[...] = jnp.where(s == n_section - 1, 0.0, built).astype(BF16)
    store(rebuilt, rebuilt_hbm)
    last[...] = dot(x[7], vg[...], TN).astype(BF16)
    store(last, gvw_hbm.at[block_of(7)])
    for copy in stores:
        copy.wait()


def on_device(n_section, layer_input, upstream, scores, value_weight, out_weight, feedback, basis):
    _, micro, length, width = layer_input.shape
    rows = micro * length
    heads = scores.shape[2]
    model, inner = value_weight.shape[1:]
    rank = basis.shape[1]
    vmem = pltpu.VMEM
    anywhere = pl.BlockSpec(memory_space=pl.ANY)
    whole = pl.BlockSpec(memory_space=vmem)
    held = pl.pallas_call(
        functools.partial(body, micro, heads, n_section),
        out_shape=(
            vmem((8, rows, width), BF16),
            vmem((8, rows, width), BF16),
            vmem((model, inner), BF16),
            vmem((micro * heads, length, length), BF16),
            vmem((rows, inner), F32),
            vmem((rows, inner), BF16),
            vmem((8, inner, width), F32),
            vmem((8, width, inner), BF16),
            vmem((rows, width), F32),
            vmem((rows, rank), BF16),
            vmem((width, rank), F32),
        ),
        in_specs=[anywhere] * 7,
        out_specs=(whole,) * 11,
        scratch_shapes=[
            vmem((inner, model), BF16),
            vmem((4, width, inner), BF16),
            vmem((micro * heads, length, length), BF16),
            vmem((rows, width), F32),
            vmem((micro * heads, length, length), BF16),
            vmem((rows, inner), F32),
            vmem((rows, inner), BF16),
            vmem((3, rows, width), F32),
            vmem((3, rows, width), BF16),
            vmem((rows, width), BF16),
            vmem((rows, width), BF16),
            vmem((rows, width), BF16),
            vmem((rows, rank), BF16),
            pltpu.SemaphoreType.DMA((7,)),
            pltpu.SemaphoreType.DMA((80,)),
            pltpu.SemaphoreType.DMA((80,)),
            pltpu.SemaphoreType.REGULAR,
        ],
        compiler_params=pltpu.CompilerParams(
            collective_id=0, has_side_effects=True, vmem_limit_bytes=40 << 20
        ),
    )(*(
        pltpu.with_memory_space_constraint(value, pltpu.HBM)
        for value in (
            layer_input.reshape(rows, width),
            upstream.reshape(rows, width),
            scores.reshape(micro * heads, length, length),
            value_weight[0],
            out_weight[0],
            feedback.reshape(rows, width),
            basis,
        )
    ))
    gow, gvw, new, rebuilt = pl.pallas_call(
        functools.partial(finish, micro, heads, n_section),
        out_shape=(
            jax.ShapeDtypeStruct((inner, model), BF16),
            jax.ShapeDtypeStruct((model, inner), BF16),
            jax.ShapeDtypeStruct((rows, width), F32),
            jax.ShapeDtypeStruct((rows, width), BF16),
        ),
        in_specs=[whole] * 11,
        out_specs=(anywhere,) * 4,
        scratch_shapes=[
            vmem((width, inner), BF16),
            vmem((8, inner, width), BF16),
            vmem((rows, inner), F32),
            vmem((rows, width), BF16),
            pltpu.SemaphoreType.DMA((18,)),
        ],
        compiler_params=pltpu.CompilerParams(vmem_limit_bytes=16 << 20),
    )(*(pltpu.with_memory_space_constraint(value, pltpu.VMEM) for value in held))
    shape = (1, micro, length, width)
    return gow[None], gvw[None], new.reshape(shape), rebuilt.reshape(shape)


def solution(mesh):
    in_specs = (
        P("section", None, None, "tensor"),
        P("section", None, None, "tensor"),
        P("section", None, "tensor", None, None),
        P("section", None, "tensor"),
        P("section", "tensor", None),
        P("section", None, None, "tensor"),
        P("tensor", None),
    )
    out_specs = (
        P("section", "tensor", None),
        P("section", None, "tensor"),
        P("section", None, None, "tensor"),
        P("section", None, None, "tensor"),
    )
    return jax.shard_map(
        functools.partial(on_device, mesh.shape["section"]),
        mesh=mesh, in_specs=in_specs, out_specs=out_specs, check_vma=False,
    )
```
